256 devices in a mesh: dp: 16 (over x, z_lo), seq: 16 (over y, z_hi, core).
Axes of the slice: x: 4, y: 4, z: 8 (z_hi: 2, z_lo: 4; z = z_hi * 4 + z_lo), core: 2. Of those that a mesh axis runs over, the one named last changes fastest.
Arguments:
- dna_ids: int32 [16, 524288], P('dp', 'seq'), may hold values from 0 to 3
- stem_weight: bfloat16 [512, 768], replicated, may hold values from -0.5 to 0.5
- kernel_taps_weight: bfloat16 [3, 768, 1536], P(None, 'dp'), may hold values from -0.125 to 0.125
- query_weight: bfloat16 [1536, 512], replicated, may hold values from -3.58237875 to 3.58237875
- key_weight: bfloat16 [1536, 128], replicated, may hold values from -0.103082693 to 0.103082693
- value_weight: bfloat16 [1536, 192], replicated, may hold values from -0.15625 to 0.15625
- out_weight: bfloat16 [1536, 768], replicated, may hold values from -0.21875 to 0.21875
- cotangent: bfloat16 [16, 4096, 1536], P('dp', 'seq'), may hold values from -6 to 6
Outputs:
- layer_out: bfloat16 [16, 4096, 1536], P('dp', 'seq')
- out_weight_grad: float32 [1536, 768], P(('dp', 'seq'))
The draws below stay inside these ranges and needn't reach their ends.
All inputs are finite; a program needn't handle non-finite values.
Results may differ from the reference program's by a relative error of at most 0.018.
Values may be sent and summed in bfloat16 or wider, within the bound.
No kernel may reach another device: no remote copies, remote signals or barrier semaphores. Data moves between devices by JAX's collectives and lax.ppermute only.
A program may use at most 128 MiB of HBM per device.

```python
import jax
import jax.numpy as jnp
from jax import lax

D0 = 768
D = 1536
HEADS = 4
HQK = 128
HV = 192
PATCH = 128
DILATION_STEP = 4
WINDOWS = 16
WINDOW_LENGTH = 4096
BASES = 524288


def shared_keys(key):
    return jnp.clip(jax.random.normal(key, (D, HQK), jnp.float32), -4.0, 4.0) * D ** (-0.5)


def draw_key_weight(key, part):
    base = shared_keys(key)
    return base.astype(jnp.bfloat16)


def draw_query_weight(key, part):
    key = jax.random.fold_in(key, 12)
    own = jnp.clip(jax.random.normal(key, (D, HEADS, HQK), jnp.float32), -4.0, 4.0) * (3.0 * D ** (-0.5))
    return own.reshape(D, HEADS * HQK).astype(jnp.bfloat16)


def with_ends(values, rng, smallest, high):
    index_at = [jax.random.randint(jax.random.fold_in(rng, axis), (), 0, length) for axis, length in enumerate(values.shape)]
    longest = values.shape.index(max(values.shape))
    neighbour = index_at[:longest] + [(index_at[longest] + 1) % values.shape[longest]] + index_at[longest + 1:]
    return values.at[tuple(index_at)].set(smallest).at[tuple(neighbour)].set(high)


def strengthened(drawn, rng, source, target, blocks, factor):
    def block_of(position):
        return (jnp.arange(drawn.shape[position]) // (drawn.shape[position] // blocks)).reshape((-1,) + (1,) * (drawn.ndim - 1 - position))

    one_side = jax.random.permutation(rng, blocks)[block_of(target)]
    far = (block_of(target) + blocks // 2) % blocks
    return jnp.where((block_of(source) == one_side) | (block_of(source) == far), factor * drawn, drawn)


def levels(own_key, dims, split, least, high):
    loudness = 1.0
    for axis_at, blocks in split:
        heights = jax.random.uniform(jax.random.fold_in(jax.random.fold_in(own_key, 6), axis_at), (blocks,), jnp.float32, least / len(split), high / len(split))
        loudness = loudness * jnp.repeat(jnp.exp(heights), dims[axis_at] // blocks).reshape((-1,) + (1,) * (len(dims) - 1 - axis_at))
    return loudness


def noise(own_key, dims, scale, most, shards=(), kind=jnp.bfloat16):
    level = levels(own_key, dims, shards, -0.22, 0.18) if shards else 1.0
    result = jax.random.normal(own_key, dims, jnp.float32) * scale * level
    return jnp.minimum(jnp.maximum(result, -most), most).astype(kind)


def bell_draw_with(rng, dims, spread, bound, shards, heavy, kind=jnp.bfloat16):
    result = spread * jax.random.normal(rng, dims, jnp.float32)
    if shards:
        result = result * levels(rng, dims, shards, -0.22, 0.18)
    return jnp.clip(strengthened(result, jax.random.fold_in(rng, 3), *heavy), -bound, bound).astype(kind)


def setup_inputs(seed: int = 0) -> dict:
    streams_of = jax.random.split(jax.random.key(seed), 9)
    return {
        "dna_ids": with_ends(jax.random.randint(streams_of[0], (WINDOWS, BASES), 0, 4), jax.random.fold_in(streams_of[0], 1), 0, 3).astype(jnp.int32),
        "stem_weight": noise(streams_of[1], (PATCH * 4, D0), PATCH ** -0.5, 0.5),
        "kernel_taps_weight": noise(streams_of[2], (3, D0, D), (3 * D0) ** -0.5, 0.125, ((1, 16),)),
        "query_weight": draw_query_weight(jax.random.fold_in(streams_of[8], 71), 0),
        "key_weight": draw_key_weight(jax.random.fold_in(streams_of[8], 71), 0),
        "value_weight": noise(streams_of[5], (D, HV), D ** -0.5, 0.15625),
        "out_weight": noise(streams_of[6], (D, HEADS * HV), (HEADS * HV) ** -0.5, 0.21875),
        "cotangent": bell_draw_with(streams_of[7], (WINDOWS, WINDOW_LENGTH, D), 1.0, 6.0, ((0, 16), (1, 16)), (1, 2, 16, 2.0)),
    }


def embed_patches(dna_ids, stem_weight):
    onehot = (dna_ids[..., None] == jnp.arange(4, dtype=jnp.int32)).astype(jnp.bfloat16)
    onehot = onehot.reshape(dna_ids.shape[0], dna_ids.shape[1], PATCH * 4)
    return jax.nn.gelu(jnp.dot(onehot, stem_weight, preferred_element_type=jnp.float32)).astype(jnp.bfloat16)

def one_window(operands):
    queries, keys_all, values_all = operands
    scores = jnp.einsum('phk,rk->hpr', queries.astype(jnp.float32), keys_all.astype(jnp.float32))
    highest = lax.optimization_barrier(jnp.max(scores, axis=-1, keepdims=True))
    expo = jnp.exp(scores - highest)
    total = lax.optimization_barrier(jnp.sum(expo, axis=-1))
    rounded = lax.optimization_barrier(expo.astype(jnp.bfloat16)).astype(jnp.float32)
    mixed = jnp.einsum('hpr,rv->phv', rounded, values_all.astype(jnp.float32))
    mixed = mixed / jnp.transpose(total)[..., None]
    return mixed.reshape(WINDOW_LENGTH, HEADS * HV).astype(jnp.bfloat16)

def reference(dna_ids, stem_weight, kernel_taps_weight, query_weight, key_weight, value_weight, out_weight, cotangent):
    stem_output = embed_patches(dna_ids.reshape(WINDOWS, WINDOW_LENGTH, PATCH), stem_weight)
    padded_input = jnp.pad(stem_output, ((0, 0), (DILATION_STEP, DILATION_STEP), (0, 0)))
    convolved_sum = jnp.zeros((WINDOWS, WINDOW_LENGTH, D), jnp.float32)
    for tap_index in range(3):
        convolved_sum = convolved_sum + jnp.dot(padded_input[:, tap_index * DILATION_STEP:tap_index * DILATION_STEP + WINDOW_LENGTH], kernel_taps_weight[tap_index], preferred_element_type=jnp.float32)
    features = jax.nn.gelu(convolved_sum).astype(jnp.bfloat16)
    wide = features.astype(jnp.float32)
    normed = (wide * lax.rsqrt(lax.optimization_barrier(jnp.mean(wide * wide, axis=-1, keepdims=True)) + 1e-06)).astype(jnp.bfloat16)
    queries = (jnp.dot(normed, query_weight, preferred_element_type=jnp.float32) * HQK ** (-0.5)).astype(jnp.bfloat16)
    queries = queries.reshape(WINDOWS, WINDOW_LENGTH, HEADS, HQK)
    keys_all = jnp.dot(normed, key_weight, preferred_element_type=jnp.float32).astype(jnp.bfloat16)
    values_all = jnp.dot(normed, value_weight, preferred_element_type=jnp.float32).astype(jnp.bfloat16)
    attn = lax.map(one_window, (queries, keys_all, values_all))
    layer_out = (wide + jnp.dot(attn, out_weight.T, preferred_element_type=jnp.float32)).astype(jnp.bfloat16)
    out_weight_grad = jnp.dot(cotangent.reshape(-1, D).T, attn.reshape(-1, HEADS * HV), preferred_element_type=jnp.float32)
    return (layer_out, out_weight_grad)
```

```python
import functools
import math

import jax
import jax.numpy as jnp
from jax import lax
from jax.experimental import pallas as pl
from jax.experimental.pallas import tpu as pltpu
from jax.sharding import PartitionSpec as P

HEADS = 4
HQK = 128
HV = 192
STEP = 4
NX, NY, NZ = 4, 4, 8
BF = jnp.bfloat16
F32 = jnp.float32

GROUPS = (
    ((0, 0), (3, 0), (1, 0), (0, 3), (0, 1)),
    ((2, 0), (0, 2), (3, 3), (3, 1), (1, 3), (1, 1)),
    ((3, 2), (1, 2), (2, 3), (2, 1), (2, 2)),
)


def flat(x, y, z, c):
    return (x * 4 + z % 4) * 16 + y * 4 + (z // 4) * 2 + c


def send(value, dx=0, dy=0, dz=0, dc=0):
    pairs = [
        (flat(x, y, z, c), flat((x + dx) % NX, (y + dy) % NY, (z + dz) % NZ, c ^ dc))
        for x in range(NX)
        for y in range(NY)
        for z in range(NZ)
        for c in range(2)
    ]
    return lax.ppermute(value, ("dp", "seq"), pairs)


def dot(a, b):
    return jnp.dot(a, b, preferred_element_type=F32)


def gather_weights(own):
    h = (own.shape[0] // 32 + 1) * 16
    w = {(0, 0): own}
    w[3, 0] = send(own, dx=1)
    w[1, 0] = send(own, dx=-1)
    w[0, 3] = send(own, dz=1)
    w[0, 1] = send(own, dz=-1)
    lo = lambda k: w[k][:h]
    hi = lambda k: w[k][h:]
    xp = send(jnp.concatenate([lo((3, 0)), lo((0, 3)), lo((0, 1))]), dx=1)
    xm = send(jnp.concatenate([hi((1, 0)), lo((0, 3)), lo((0, 1))]), dx=-1)
    zp = send(jnp.concatenate([lo((0, 3)), hi((3, 0)), hi((1, 0))]), dz=1)
    zm = send(jnp.concatenate([hi((0, 1)), hi((3, 0)), hi((1, 0))]), dz=-1)
    e = own.shape[0] - h
    cat = lambda *a: jnp.concatenate(a)
    w[2, 0] = cat(xp[:h], xm[:e])
    w[0, 2] = cat(zp[:h], zm[:e])
    w[3, 3] = cat(xp[h : 2 * h], zp[h : h + e])
    w[3, 1] = cat(xp[2 * h :], zm[e : 2 * e])
    w[1, 3] = cat(xm[e : e + h], zp[h + e :])
    w[1, 1] = cat(xm[e + h :], zm[2 * e :])
    w[3, 2] = send(w[0, 2], dx=1)
    w[1, 2] = send(w[0, 2], dx=-1)
    w[2, 3] = send(w[2, 0], dz=1)
    w[2, 1] = send(w[2, 0], dz=-1)
    q = own.shape[0] // 64 * 16
    w[2, 2] = cat(
        send(w[3, 2][:q], dx=1),
        send(w[1, 2][q : 2 * q], dx=-1),
        send(w[2, 3][2 * q : 3 * q], dz=1),
        send(w[2, 1][3 * q :], dz=-1),
    )
    return w


def attend_kernel(n_kv, first, last, *refs):
    q_ref, kvs = refs[0], refs[1 : 1 + n_kv]
    rest = refs[1 + n_kv :]
    if not first:
        m_in, acc_in = rest[:2]
        rest = rest[2:]
    rows = q_ref.shape[0]
    for h in range(HEADS):
        q = q_ref[:, h * HQK : (h + 1) * HQK]
        scores = [
            lax.dot_general(
                q, kv[:, :HQK], (((1,), (1,)), ((), ())), preferred_element_type=F32
            )
            for kv in kvs
        ]
        top = functools.reduce(
            jnp.maximum, [jnp.max(s, axis=1, keepdims=True) for s in scores]
        )
        here = pl.ds(h * rows, rows)
        if not first:
            before = m_in[here, :1]
            top = jnp.maximum(top, before)
        total = None
        for s, kv in zip(scores, kvs):
            p = jnp.exp2(s - top).astype(BF)
            part = dot(p, kv[:, HQK:])
            total = part if total is None else total + part
        if not first:
            total = total + acc_in[here, :] * jnp.exp2(before - top)
        if last:
            out_ref = rest[0]
            norm = total[:, :HV] / total[:, HV : HV + 1]
            out_ref[:, h * HV : (h + 1) * HV] = norm.astype(BF)
        else:
            m_out, acc_out = rest
            m_out[here, :] = jnp.broadcast_to(top, (rows, 128))
            acc_out[here, :] = total


def attend(q, kvs, state, last):
    rows = q.shape[0]
    if last:
        out = jax.ShapeDtypeStruct((rows, HEADS * HV), BF)
    else:
        out = (
            jax.ShapeDtypeStruct((HEADS * rows, 128), F32),
            jax.ShapeDtypeStruct((HEADS * rows, 256), F32),
        )
    n = sum(kv.shape[0] for kv in kvs)
    return pl.pallas_call(
        functools.partial(attend_kernel, len(kvs), not state, last),
        out_shape=out,
        compiler_params=pltpu.CompilerParams(vmem_limit_bytes=48 << 20),
        cost_estimate=pl.CostEstimate(
            flops=2 * HEADS * rows * n * 512,
            bytes_accessed=n * 768,
            transcendentals=HEADS * rows * n,
        ),
    )(q, *kvs, *state)


def local(
    dna_ids,
    stem_weight,
    kernel_taps_weight,
    query_weight,
    key_weight,
    value_weight,
    out_weight,
    cotangent,
):
    patch = stem_weight.shape[0] // 4
    d0 = stem_weight.shape[1]
    n_pos = dna_ids.shape[1] // patch
    share = kernel_taps_weight.shape[1]
    width = kernel_taps_weight.shape[2]
    half = width // 2
    dp, seq = lax.axis_index("dp"), lax.axis_index("seq")
    x, zl = dp // 4, dp % 4
    y, zh, c = seq // 4, (seq // 2) % 2, seq % 2
    z = zh * 4 + zl

    taps = kernel_taps_weight.reshape(3 * share, width)
    mine = lax.dynamic_slice_in_dim(taps, c * half, half, axis=1)
    parts = [
        gather_weights(mine[:, : half // 2]),
        gather_weights(mine[:, half // 2 :]),
    ]

    own = dna_ids.reshape(n_pos, patch).astype(BF)
    beside = send(own, dc=1)
    far = send(own, dz=4)
    far_beside = send(far, dc=1)
    order = lambda a, b, k: jnp.where(k == 0, jnp.stack([a, b]), jnp.stack([b, a]))
    near2 = order(own, beside, c)
    far2 = order(far, far_beside, c)
    whole = order(near2, far2, zh).reshape(4 * n_pos, patch)
    none = jnp.full((STEP, patch), -1, BF)
    before = jnp.where(y == 0, none, send(whole[-STEP:], dy=1))
    after = jnp.where(y == NY - 1, none, send(whole[:STEP], dy=-1))
    ext = jnp.concatenate([before, whole, after])

    sw = stem_weight.reshape(patch, 4, d0).transpose(1, 0, 2).reshape(4 * patch, d0)
    chan = lax.broadcasted_iota(jnp.int32, (d0, d0), 0)
    flat_offsets = [o for g in GROUPS for o in g]
    starts = jnp.stack([(((x + ox) % 4) * 4 + (zl + oz) % 4) * share for ox, oz in flat_offsets])
    wanted = (starts[:, None] + jnp.arange(share)[None, :]).reshape(1, d0)
    sw = dot(sw, (chan == wanted).astype(BF)).astype(BF)

    blocks = [zh * 2 + 1 - c, (1 - zh) * 2 + 1 - c, zh * 2 + c, (1 - zh) * 2 + c]
    xs = [[] for _ in GROUPS]
    for t in range(3):
        ids = ext[t * STEP : t * STEP + 4 * n_pos].reshape(4, n_pos, patch)
        ids = jnp.concatenate(
            [lax.dynamic_index_in_dim(ids, b, 0, keepdims=False) for b in blocks]
        )
        onehot = jnp.concatenate([(ids == b).astype(BF) for b in range(4)], axis=1)
        at = 0
        for g, group in enumerate(GROUPS):
            n = share * len(group)
            xs[g].append(jax.nn.gelu(dot(onehot, sw[:, at : at + n])).astype(BF))
            at += n
    xs = [jnp.concatenate(v, axis=1) for v in xs]

    rows_each = width // 256
    r = jnp.arange(half)
    j, kz = r % rows_each, (r // rows_each) % 8
    kx, ky = (r // (rows_each * 8)) % 4, r // (rows_each * 32)
    rx, ry, rz = (x + kx) % 4, (y + ky) % 4, (z + kz) % 8
    base = ((rx * 4 + rz % 4) * 16 + ry * 4 + (rz // 4) * 2) * rows_each + j
    col = lax.broadcasted_iota(jnp.int32, (width, half), 0)
    cot = cotangent[0]
    cot_keep = dot(cot, (col == (base + c * rows_each)[None]).astype(BF)).astype(BF)
    cot_send = dot(cot, (col == (base + (1 - c) * rows_each)[None]).astype(BF)).astype(BF)
    cot2 = jnp.concatenate([cot_keep, send(cot_send, dc=1)])

    wkv = jnp.concatenate(
        [key_weight, value_weight, jnp.zeros((width, 384 - HQK - HV), BF)], axis=1
    )
    pick = lambda w, k: lax.dynamic_slice_in_dim(w, k * half, half, axis=0)
    wkv_c, wkv_o = pick(wkv, c), pick(wkv, 1 - c)
    wq_c, wq_o = pick(query_weight, c), pick(query_weight, 1 - c)
    wo_c, wo_o = pick(out_weight, c), pick(out_weight, 1 - c)

    def weights_of(part, group):
        return jnp.concatenate(
            [part[o][t * share : (t + 1) * share] for t in range(3) for o in group]
        )

    def conv(lo, hi):
        cols = []
        for part in parts:
            acc = dot(xs[0][lo:hi], weights_of(part, GROUPS[0]))
            acc = acc + dot(xs[1][lo:hi], weights_of(part, GROUPS[1]))
            acc = acc + dot(xs[2][lo:hi], weights_of(part, GROUPS[2]))
            cols.append(jax.nn.gelu(acc).astype(BF))
        return jnp.concatenate(cols, axis=1)

    f_recv = send(conv(0, 2 * n_pos), dc=1)
    f_keep = conv(2 * n_pos, 4 * n_pos)

    wide_k, wide_r = f_keep.astype(F32), f_recv.astype(F32)
    squares = jnp.sum(wide_k * wide_k, -1, keepdims=True) + jnp.sum(wide_r * wide_r, -1, keepdims=True)
    scale = lax.rsqrt(squares / width + 1e-06)
    n_keep, n_recv = (wide_k * scale).astype(BF), (wide_r * scale).astype(BF)
    kv = dot(n_keep, wkv_c) + dot(n_recv, wkv_o)
    lane = lax.broadcasted_iota(jnp.int32, (1, 384), 1)
    kv = jnp.where(lane == HQK + HV, 1.0, kv).astype(BF)
    q = dot(n_keep[:n_pos], wq_c) + dot(n_recv[:n_pos], wq_o)
    q = (q * (HQK ** (-0.5) * math.log2(math.e))).astype(BF)

    kv1 = send(kv, dy=1)
    kv3 = send(kv, dy=-1)
    kv_o = send(kv, dc=1)
    kv2a = send(kv1[:n_pos], dy=1)
    kv2b = send(kv3[n_pos:], dy=-1)
    kv1_o, kv3_o = send(kv1, dc=1), send(kv3, dc=1)
    kv2a_o, kv2b_o = send(kv2a, dc=1), send(kv2b, dc=1)
    state = attend(q, [kv, kv_o], (), False)
    state = attend(q, [kv1, kv1_o, kv3, kv3_o], state, False)
    attn = attend(q, [kv2a, kv2b, kv2a_o, kv2b_o], state, True)

    attn2 = jnp.concatenate([attn, send(attn, dc=1)])
    grad = lax.dot_general(cot2, attn2, (((0,), (0,)), ((), ())), preferred_element_type=F32)

    cols = grad.shape[1] // 2
    shape = (4, 4, 8 * rows_each, cols)
    left = grad[:, :cols].reshape(shape)
    right = grad[:, cols:].reshape(shape)

    def ring(take, axis):
        got = take(0)
        for k, d in ((2, 2), (1, 1), (3, -1)):
            got = got + send(take(k).astype(BF), **{axis: d}).astype(F32)
        return got

    left1, right1 = left, right
    left2 = ring(lambda k: left1[k], "dy")
    right2 = ring(lambda k: right1[:, k], "dx")
    left = ring(lambda k: left2[k], "dx")
    right = ring(lambda k: right2[k], "dy")
    both = jnp.concatenate([left, right], axis=1).reshape(8, rows_each, 2 * cols)
    out_grad = both[0]
    for k in (4, 3, 5, 2, 6, 1, 7):
        out_grad = out_grad + send(both[k].astype(BF), dz=k).astype(F32)

    home_c = f_keep[:n_pos].astype(F32) + lax.dot_general(
        attn, wo_c, (((1,), (1,)), ((), ())), preferred_element_type=F32
    )
    home_o = f_recv[:n_pos].astype(F32) + lax.dot_general(
        attn, wo_o, (((1,), (1,)), ((), ())), preferred_element_type=F32
    )
    home_c, home_o = home_c.astype(BF), home_o.astype(BF)
    layer_out = jnp.where(
        c == 0,
        jnp.concatenate([home_c, home_o], axis=1),
        jnp.concatenate([home_o, home_c], axis=1),
    )
    return (layer_out[None], out_grad)


def solution(mesh):
    placed = (P("dp", "seq"), P(), P(None, "dp", None), P(), P(), P(), P(), P("dp", "seq", None))
    return jax.shard_map(
        local,
        mesh=mesh,
        in_specs=placed,
        out_specs=(P("dp", "seq", None), P(("dp", "seq"), None)),
        check_vma=False,
    )
```

```python
import functools
import math

import jax
import jax.numpy as jnp
from jax import lax
from jax.experimental import pallas as pl
from jax.experimental.pallas import tpu as pltpu
from jax.sharding import PartitionSpec as P

HEADS = 4
HQK = 128
HV = 192
STEP = 4
NX, NY, NZ = 4, 4, 8
BF = jnp.bfloat16
F32 = jnp.float32

FIRST = ((0, 0), (3, 0), (1, 0), (2, 0), (0, 3), (0, 1), (0, 2))
SECOND = ((3, 2), (3, 1), (3, 3), (1, 2), (1, 1), (1, 3), (2, 3), (2, 1), (2, 2))
CUT = 32


def flat(x, y, z, c):
    return (x * 4 + z % 4) * 16 + y * 4 + (z // 4) * 2 + c


def route(value, target):
    places = [(x, y, z, c) for x in range(NX) for y in range(NY) for z in range(NZ) for c in range(2)]
    pairs = [(flat(*p), flat(*target(*p))) for p in places if target(*p)]
    return lax.ppermute(value, ("dp", "seq"), pairs)


def send(value, dx=0, dy=0, dz=0, dc=0):
    return route(
        value, lambda x, y, z, c: ((x + dx) % NX, (y + dy) % NY, (z + dz) % NZ, c ^ dc)
    )


def two_away(value):
    return route(value, lambda x, y, z, c: (x, y, (z + 2 - 4 * c) % NZ, c))


def to_ends(value, swapped):
    def target(x, y, z, c):
        if z // 4 != c:
            return None
        z, e = ((z + 4) % NZ, 1 - c) if swapped else (z, c)
        return x, (y + 2 * c - 1) % NY, z, e

    return route(value, target)


def dot(a, b):
    return jnp.dot(a, b, preferred_element_type=F32)


def dot_t(a, b):
    return lax.dot_general(a, b, (((1,), (1,)), ((), ())), preferred_element_type=F32)


def params():
    return pltpu.CompilerParams(vmem_limit_bytes=20 << 20)


def cost(flops, moved=1 << 20, exps=0):
    return pl.CostEstimate(flops=flops, bytes_accessed=moved, transcendentals=exps)


SMEM = pl.BlockSpec(memory_space=pltpu.SMEM)
VMEM = pl.BlockSpec(memory_space=pltpu.VMEM)


def shape(*dims, dtype=BF):
    return jax.ShapeDtypeStruct(dims, dtype)


def prep_kernel(starts, sw_ref, first_ref, second_ref):
    n_rows, d0 = sw_ref.shape
    share = d0 // (len(FIRST) + len(SECOND))
    to = lax.broadcasted_iota(jnp.int32, (n_rows, n_rows), 0)
    of = lax.broadcasted_iota(jnp.int32, (n_rows, n_rows), 1)
    patch = n_rows // 4
    rows = jnp.where(of == (to % patch) * 4 + to // patch, 1.0, 0.0).astype(BF)
    sw = dot(rows, sw_ref[...]).astype(BF)
    at = 0
    for group, out_ref in ((FIRST, first_ref), (SECOND, second_ref)):
        n = share * len(group)
        lane = lax.broadcasted_iota(jnp.int32, (1, n), 1)
        wanted = jnp.zeros((1, n), jnp.int32)
        for i in range(len(group)):
            here = (lane >= i * share) & (lane < (i + 1) * share)
            wanted = jnp.where(here, starts[at + i] + lane - i * share, wanted)
        chan = lax.broadcasted_iota(jnp.int32, (d0, n), 0)
        out_ref[...] = dot(sw, jnp.where(chan == wanted, 1.0, 0.0).astype(BF)).astype(BF)
        at += len(group)


def stem_kernel(place, pair_ref, other_ref, sw1_ref, sw2_ref, *rest):
    outs, ext = rest[:-1], rest[-1]
    n_pos = (pair_ref.shape[0] - 16) // 2
    y, zh, c = place[0], place[1], place[2]
    edge = jnp.full((STEP, ext.shape[1]), -1.0, F32)
    ends = jnp.where(zh == c, pair_ref[2 * n_pos :, :], other_ref[2 * n_pos :, :]).astype(F32)
    ends = jnp.where(
        zh == 0, ends[:8], jnp.concatenate([ends[STEP:8], ends[:STEP]])
    )
    first = jnp.where(y == 0, edge, ends[:STEP])
    last = jnp.where(y == NY - 1, edge, ends[STEP:])
    ext[0:8, :] = jnp.concatenate([edge, first])
    ext[8 + 4 * n_pos :, :] = jnp.concatenate([last, edge])
    blocks = [zh * 2 + c, (1 - zh) * 2 + c, zh * 2 + 1 - c, (1 - zh) * 2 + 1 - c]
    for i, b in enumerate(blocks):
        ref = (pair_ref, other_ref)[i // 2]
        block = ref[i % 2 * n_pos : (i % 2 + 1) * n_pos, :]
        ext[pl.ds(pl.multiple_of(8 + b * n_pos, 8), n_pos), :] = block.astype(F32)
    n = n_pos + 16
    for i, b in enumerate(blocks[2:] + blocks[:2]):
        ids = ext[pl.ds(pl.multiple_of(b * n_pos, 8), n), :]
        onehot = jnp.concatenate(
            [jnp.where(ids == k, 1.0, 0.0).astype(BF) for k in range(4)], axis=1
        )
        for g, sw_ref in enumerate((sw1_ref, sw2_ref)):
            stem = jax.nn.gelu(dot(onehot, sw_ref[...]))
            for t in range(3):
                at = STEP * (t + 1)
                outs[g * 3 + t][i * n_pos : (i + 1) * n_pos, :] = stem[at : at + n_pos].astype(BF)


def tap_weights(pieces, t):
    share = pieces[0].shape[0] // 3
    return jnp.concatenate([p[t * share : (t + 1) * share] for p in pieces])


def conv1_kernel(x0, x1, x2, *rest):
    pieces = [r[...] for r in rest[:7]]
    step = x0.shape[0] // 4

    def body(i, _):
        here = pl.ds(pl.multiple_of(i * step, step), step)
        total = None
        for t, x in enumerate((x0, x1, x2)):
            part = dot(x[here, :], tap_weights(pieces, t))
            total = part if total is None else total + part
        rest[-1][here, :] = total
        return 0

    lax.fori_loop(0, 4, body, 0)


def conv2_kernel(part, acc, x0, x1, x2, fx, fxm, fz, fzm, fx2, out):
    n = fx2.shape[0]
    xa, xb, za, zb = fx[...], fxm[...], fz[...], fzm[...]
    u = n - CUT
    cat = lambda a, b: jnp.concatenate([a, b])
    pieces = [
        xa[:n],
        cat(xa[n : n + CUT], zb[n : n + u]),
        cat(xa[n + CUT :], za[n : n + u]),
        xb[:n],
        cat(xb[n : n + CUT], zb[n + u :]),
        cat(xb[n + CUT :], za[n + u :]),
        za[:n],
        zb[:n],
        fx2[...],
    ]
    rows = out.shape[0] // 2
    for i in range(2):
        here = pl.ds((2 * part + i) * rows, rows)
        total = acc[here, :]
        for t, x in enumerate((x0, x1, x2)):
            total = total + dot(x[here, :], tap_weights(pieces, t))
        out[i * rows : (i + 1) * rows, :] = jax.nn.gelu(total).astype(BF)


def conv1(xs, pieces):
    rows, cols = xs[0].shape[0], pieces[0].shape[1]
    return pl.pallas_call(
        conv1_kernel,
        out_shape=shape(rows, cols, dtype=F32),
        compiler_params=params(),
        cost_estimate=cost(6 * rows * xs[0].shape[1] * cols, 7 << 20),
    )(*xs, *pieces)


def conv2(acc, xs, pieces, part):
    rows, cols = acc.shape
    return pl.pallas_call(
        functools.partial(conv2_kernel, part),
        out_shape=shape(rows // 2, cols),
        compiler_params=params(),
        cost_estimate=cost(3 * rows * xs[0].shape[1] * cols, 4 << 20),
    )(acc, *xs, *pieces)


def project_kernel(sel, fk, fr, wq, wk, wv, q_mine, q_send, kv_out):
    n_pos, half, qc = fk.shape[0] // 2, fk.shape[1], wq.shape[1] // 2
    c = sel[0]
    my, other = [pl.ds(pl.multiple_of(k * half, half), half) for k in (c, 1 - c)]
    mine, theirs = [pl.ds(pl.multiple_of(k * qc, qc), qc) for k in (c, 1 - c)]
    wide_k, wide_r = fk[...].astype(F32), fr[...].astype(F32)
    squares = jnp.sum(wide_k * wide_k, -1, keepdims=True)
    squares = squares + jnp.sum(wide_r * wide_r, -1, keepdims=True)
    scale = lax.rsqrt(squares / (2 * half) + 1e-06)
    nk, nr = (wide_k * scale).astype(BF), (wide_r * scale).astype(BF)
    factor = HQK ** (-0.5) * math.log2(math.e)
    hk, hr = nk[:n_pos], nr[:n_pos]
    q_send[...] = ((dot(hk, wq[my, theirs]) + dot(hr, wq[other, theirs])) * factor).astype(BF)
    q_mine[...] = ((dot(hk, wq[my, mine]) + dot(hr, wq[other, mine])) * factor).astype(BF)
    n = 2 * n_pos
    kv_out[:n, :] = (dot(nk, wk[my, :]) + dot(nr, wk[other, :])).astype(BF)
    v = dot_t(nk, wv[:, my]) + dot_t(nr, wv[:, other])
    kv_out[n : 2 * n, :] = v[:, :128].astype(BF)
    tail = v[:, 128:]
    kv_out[2 * n :, :] = jnp.concatenate([tail[:n_pos], tail[n_pos:]], axis=1).astype(BF)


def project(c, f_keep, f_recv, query_weight, key_weight, value_weight):
    n, half = f_keep.shape
    n_pos = n // 2
    qc = query_weight.shape[1] // 2
    return pl.pallas_call(
        project_kernel,
        in_specs=[SMEM] + [VMEM] * 5,
        out_shape=[shape(n_pos, qc), shape(n_pos, qc), shape(5 * n_pos, 128)],
        compiler_params=params(),
        cost_estimate=cost(4 * n * half * 640, 4 << 20),
    )(c, f_keep, f_recv, query_weight, key_weight, value_weight)


def unpack(packed):
    n = packed.shape[0] // 5
    k, va, tail = packed[: 2 * n], packed[2 * n : 4 * n], packed[4 * n :]
    tail = tail.astype(F32)
    tail = jnp.concatenate([tail, pltpu.roll(tail, 64, 1)])
    lane = lax.broadcasted_iota(jnp.int32, tail.shape, 1)
    tail = jnp.where(lane < HV - 128, tail, jnp.where(lane == HV - 128, 1.0, 0.0))
    return k, jnp.concatenate([va, tail.astype(BF)], axis=1)


def attend_kernel(groups, first, last, *refs):
    qs = refs[:2]
    at = 2
    kvs = []
    for n in groups:
        kvs.append(unpack(jnp.concatenate([r[...] for r in refs[at : at + n]])))
        at += n
    rest = refs[at:]
    if not first:
        m_in, acc_in = rest[:2]
        rest = rest[2:]
    rows = qs[0].shape[0]
    for w in range(2):
        for h in range(HEADS // 2):
            q = qs[w][:, h * HQK : (h + 1) * HQK]
            scores = [dot_t(q, k) for k, _ in kvs]
            top = functools.reduce(
                jnp.maximum, [jnp.max(s, axis=1, keepdims=True) for s in scores]
            )
            here = pl.ds((w * 2 + h) * rows, rows)
            if not first:
                before = m_in[here, :1]
                top = jnp.maximum(top, before)
            total = None
            for s, (_, v) in zip(scores, kvs):
                part = dot(jnp.exp2(s - top).astype(BF), v)
                total = part if total is None else total + part
            if not first:
                total = total + acc_in[here, :] * jnp.exp2(before - top)
            if last:
                norm = total[:, :HV] / total[:, HV : HV + 1]
                rest[0][w * rows : (w + 1) * rows, h * HV : (h + 1) * HV] = norm.astype(BF)
            else:
                rest[0][here, :] = jnp.broadcast_to(top, (rows, 128))
                rest[1][here, :] = total


def attend(qs, kvs, state, last):
    rows = qs[0].shape[0]
    if last:
        out = shape(2 * rows, HEADS // 2 * HV)
    else:
        out = (shape(4 * rows, 128, dtype=F32), shape(4 * rows, 256, dtype=F32))
    n = sum(kv.shape[0] for group in kvs for kv in group) * 2 // 5
    return pl.pallas_call(
        functools.partial(attend_kernel, tuple(len(g) for g in kvs), not state, last),
        out_shape=out,
        compiler_params=params(),
        cost_estimate=cost(8 * rows * n * 512, n * 768, 4 * rows * n),
    )(*qs, *[kv for group in kvs for kv in group], *state)


def finish_kernel(sel, fk, fr, attn, theirs, w, out):
    n_pos, cols = theirs.shape
    half = fk.shape[1]
    c = sel[0]
    mine, other = [pl.ds(pl.multiple_of(k * cols, cols), cols) for k in (c, 1 - c)]
    a, b = attn[:n_pos, :], theirs[...]
    ours, far = fk[:n_pos, :].astype(F32), fr[:n_pos, :].astype(F32)
    for k in range(2):
        rows = slice(k * half, (k + 1) * half)
        total = jnp.where(c == k, ours, far) + dot_t(a, w[rows, mine]) + dot_t(b, w[rows, other])
        out[:, rows] = total.astype(BF)


def finish(c, f_keep, f_recv, attn, theirs, out_weight):
    n_pos, cols = theirs.shape
    width = out_weight.shape[0]
    return pl.pallas_call(
        finish_kernel,
        in_specs=[SMEM] + [VMEM] * 5,
        out_shape=shape(n_pos, width),
        compiler_params=params(),
        cost_estimate=cost(4 * n_pos * width * cols, 4 << 20),
    )(c, f_keep, f_recv, attn, theirs, out_weight)


def grad_kernel(at, cot, cot_far, attn, own, one, two, three):
    n_pos, block = cot.shape[0], own.shape[0]
    a, b = attn[:n_pos, :], attn[n_pos:, :]
    down = lambda u, v: lax.dot_general(u, v, (((0,), (0,)), ((), ())), preferred_element_type=F32)
    for k, out in ((2, two), (1, one), (3, three), (0, own)):
        here = pl.ds(pl.multiple_of(((at[0] + k) % 4) * block, block), block)
        out[...] = (down(cot[:, here], a) + down(cot_far[:, here], b)).astype(out.dtype)


def gradient(x, cot, cot_far, attn):
    block, cols = cot.shape[1] // 4, attn.shape[1]
    return pl.pallas_call(
        grad_kernel,
        in_specs=[SMEM] + [VMEM] * 3,
        out_shape=[shape(block, cols, dtype=F32)] + [shape(block, cols)] * 3,
        compiler_params=params(),
        cost_estimate=cost(16 * cot.shape[0] * block * cols, 3 << 20),
    )(x, cot, cot_far, attn)


def split_y_kernel(at, own, a, b, d, mine, one, two, three, total):
    total[...] = own[...] + a[...].astype(F32) + b[...].astype(F32) + d[...].astype(F32)
    n = mine.shape[0] // 4
    for k, out in ((2, two), (1, one), (3, three), (0, mine)):
        y = (at[1] + k) % 4
        for zl in range(4):
            rows = pl.ds(pl.multiple_of((zl * 4 + y) * n, 8), n)
            out[zl * n : (zl + 1) * n, :] = total[rows, :].astype(out.dtype)


def split_y(at, own, came):
    rows, cols = own.shape
    return pl.pallas_call(
        split_y_kernel,
        in_specs=[SMEM] + [VMEM] * 4,
        out_shape=[shape(rows // 4, cols, dtype=F32)] + [shape(rows // 4, cols)] * 3,
        scratch_shapes=[pltpu.VMEM((rows, cols), F32)],
        compiler_params=params(),
        cost_estimate=cost(rows * cols * 4),
    )(at, own, *came)


def split_z_kernel(own, a, b, d, out):
    total = own[...] + a[...].astype(F32) + b[...].astype(F32) + d[...].astype(F32)
    n = out.shape[1]
    for zl in range(4):
        for zh in range(2):
            at = (zl * 2 + zh) * n
            out[zh * 4 + zl] = total[at : at + n].astype(BF)


def split_z(own, came):
    rows, cols = own.shape
    return pl.pallas_call(
        split_z_kernel,
        in_specs=[VMEM] * 4,
        out_shape=shape(8, rows // 8, cols),
        compiler_params=params(),
        cost_estimate=cost(rows * cols * 4),
    )(own, *came)


def gather_kernel(sel, came, keep, away):
    total = jnp.sum(came[...].astype(F32), axis=0)
    n = total.shape[0] // 2
    keep[...] = jnp.where(sel[0] == 0, total[:n], total[n:])
    away[...] = jnp.where(sel[0] == 0, total[n:], total[:n])


def gathered(c, came):
    _, rows, cols = came.shape
    return pl.pallas_call(
        gather_kernel,
        in_specs=[SMEM, VMEM],
        out_shape=[shape(rows // 2, cols, dtype=F32)] * 2,
        compiler_params=params(),
        cost_estimate=cost(rows * cols * 32),
    )(c, came)


def half_kernel(sel, taps, out):
    out[...] = taps[...]


def my_half(c, taps):
    rows, width = taps.shape
    return pl.pallas_call(
        half_kernel,
        grid_spec=pltpu.PrefetchScalarGridSpec(
            num_scalar_prefetch=1,
            grid=(1,),
            in_specs=[pl.BlockSpec((rows, width // 2), lambda i, s: (0, s[0]))],
            out_specs=pl.BlockSpec((rows, width // 2), lambda i, s: (0, 0)),
        ),
        out_shape=shape(rows, width // 2),
        compiler_params=params(),
        cost_estimate=cost(0, rows * width * 2),
    )(c, taps)


def local(
    dna_ids,
    stem_weight,
    kernel_taps_weight,
    query_weight,
    key_weight,
    value_weight,
    out_weight,
    cotangent,
):
    patch = stem_weight.shape[0] // 4
    n_pos = dna_ids.shape[1] // patch
    share, width = kernel_taps_weight.shape[1:]
    dp, seq = lax.axis_index("dp"), lax.axis_index("seq")
    x, zl = dp // 4, dp % 4
    y, zh, c = seq // 4, (seq // 2) % 2, seq % 2
    core = c.astype(jnp.int32).reshape(1)
    cat = lambda *a: jnp.concatenate(a)

    own = my_half(core, kernel_taps_weight.reshape(3 * share, width))
    wx, wxm = send(own, dx=1), send(own, dx=-1)
    wz, wzm = send(own, dz=1), send(own, dz=-1)

    wx2, wz2 = send(own, dx=2), two_away(own)

    ids = dna_ids.reshape(n_pos, patch).astype(BF)
    far = send(ids, dz=4)
    end = jnp.where(c == 1, ids[-STEP:], ids[:STEP])
    ends = [to_ends(end, True), to_ends(end, False)]
    pair = cat(ids, far, *ends, jnp.zeros((16 - 2 * STEP, patch), BF))
    pair, wx, wxm, wz, wzm = lax.optimization_barrier((pair, wx, wxm, wz, wzm))
    other = send(pair, dc=1)

    starts = jnp.stack(
        [(((x + ox) % 4) * 4 + (zl + oz) % 4) * share for ox, oz in FIRST + SECOND]
    ).astype(jnp.int32)
    n1, n2 = share * len(FIRST), share * len(SECOND)
    sw1, sw2 = pl.pallas_call(
        prep_kernel,
        in_specs=[SMEM, VMEM],
        out_shape=[shape(4 * patch, n1), shape(4 * patch, n2)],
        compiler_params=params(),
        cost_estimate=cost(10**9),
    )(starts, stem_weight)
    xs = pl.pallas_call(
        stem_kernel,
        in_specs=[SMEM] + [VMEM] * 4,
        out_shape=[shape(4 * n_pos, n1)] * 3 + [shape(4 * n_pos, n2)] * 3,
        scratch_shapes=[pltpu.VMEM((4 * n_pos + 16, patch), F32)],
        compiler_params=params(),
        cost_estimate=cost(3 * 10**9, 8 << 20),
    )(jnp.stack([y, zh, c]).astype(jnp.int32), pair, other, sw1, sw2)

    px = cat(wz2, wzm[:CUT], wz[:CUT])
    pz = cat(wx2, wx[CUT:], wxm[CUT:])
    fx, fxm = send(px, dx=1), send(px, dx=-1)
    fz, fzm = send(pz, dz=1), send(pz, dz=-1)
    fx2 = send(px[: 3 * share], dx=2)
    cot = cotangent[0]
    cot_far = send(cot, dc=1)

    acc = conv1(xs[:3], [own, wx, wxm, wx2, wz, wzm, wz2])
    pieces = [fx, fxm, fz, fzm, fx2]
    f_recv = send(conv2(acc, xs[3:], pieces, 0), dc=1)
    f_keep = conv2(acc, xs[3:], pieces, 1)
    q_mine, q_send, kv = project(core, f_keep, f_recv, query_weight, key_weight, value_weight.T)

    kv1, kv3, kv2 = send(kv, dy=1), send(kv, dy=-1), send(kv, dy=2)
    qs = [q_mine, send(q_send, dc=1)]
    kv_o = send(kv, dc=1)
    state = attend(qs, [[kv], [kv_o]], (), False)
    kv1, kv2, kv3, *state = lax.optimization_barrier((kv1, kv2, kv3, *state))
    kv1_o, kv3_o, kv2_o = send(kv1, dc=1), send(kv3, dc=1), send(kv2, dc=1)
    state = attend(qs, [[kv1], [kv3], [kv2]], state, False)
    attn = attend(qs, [[kv1_o], [kv3_o], [kv2_o]], state, True)

    at = jnp.stack([x, y]).astype(jnp.int32)
    own_part, *parts = gradient(at, cot, cot_far, attn)
    came = [send(parts[k - 1], dx=k) for k in (2, 1, 3)]
    attn, *parts = lax.optimization_barrier((attn, *parts))
    theirs = send(attn[n_pos:], dc=1)
    layer_out = finish(core, f_keep, f_recv, attn, theirs, out_weight)
    layer_out, *came = lax.optimization_barrier((layer_out, *came))
    own_part, *parts = split_y(at, own_part, came)
    came = [send(parts[k - 1], dy=k) for k in (2, 1, 3)]
    chunks = split_z(own_part, came)
    groups = [
        [flat(i, j, k, m) for k in range(NZ)]
        for i in range(NX)
        for j in range(NY)
        for m in range(2)
    ]
    came = lax.all_to_all(chunks, ("dp", "seq"), 0, 0, axis_index_groups=groups)
    keep, away = gathered(core, came)
    away = send(away, dc=1)
    out_grad = jnp.where(
        c == 0,
        jnp.concatenate([keep, away], axis=1),
        jnp.concatenate([away, keep], axis=1),
    )
    return (layer_out[None], out_grad)


def solution(mesh):
    placed = (P("dp", "seq"), P(), P(None, "dp", None), P(), P(), P(), P(), P("dp", "seq", None))
    return jax.shard_map(
        local,
        mesh=mesh,
        in_specs=placed,
        out_specs=(P("dp", "seq", None), P(("dp", "seq"), None)),
        check_vma=False,
    )
```

```python
import functools
import math

import jax
import jax.numpy as jnp
from jax import lax
from jax.experimental import pallas as pl
from jax.experimental.pallas import tpu as pltpu
from jax.sharding import PartitionSpec as P

HEADS = 4
HQK = 128
HV = 192
STEP = 4
NX, NY, NZ = 4, 4, 8
BF = jnp.bfloat16
F32 = jnp.float32

FIRST = ((0, 0), (3, 0), (1, 0), (2, 0), (0, 3), (0, 1), (0, 2))
SECOND = ((3, 2), (3, 3), (3, 1), (1, 2), (1, 3), (1, 1), (2, 3), (2, 1), (2, 2))


def flat(x, y, z, c):
    return (x * 4 + z % 4) * 16 + y * 4 + (z // 4) * 2 + c


def route(value, target):
    places = [(x, y, z, c) for x in range(NX) for y in range(NY) for z in range(NZ) for c in range(2)]
    pairs = [(flat(*p), flat(*target(*p))) for p in places if target(*p)]
    return lax.ppermute(value, ("dp", "seq"), pairs)


def send(value, dx=0, dy=0, dz=0, dc=0):
    return route(
        value, lambda x, y, z, c: ((x + dx) % NX, (y + dy) % NY, (z + dz) % NZ, c ^ dc)
    )


def cores(value, first, second, by):
    def target(x, y, z, c):
        to = {"x": x, "y": y, "z": z}
        axis = (first, second)[c]
        step = -by if axis == "z" and by == 2 and z % 2 else by
        to[axis] = (to[axis] + step) % {"x": NX, "y": NY, "z": NZ}[axis]
        return to["x"], to["y"], to["z"], c

    return route(value, target)


def round_ring(value, up=1):
    return route(value, lambda x, y, z, c: (x, (y + up * (1 - 2 * c)) % NY, z, c))


def dot(a, b):
    return jnp.dot(a, b, preferred_element_type=F32)


def dot_t(a, b):
    return lax.dot_general(a, b, (((1,), (1,)), ((), ())), preferred_element_type=F32)


def params():
    return pltpu.CompilerParams(vmem_limit_bytes=20 << 20)


def cost(flops, moved=1 << 20, exps=0):
    return pl.CostEstimate(flops=flops, bytes_accessed=moved, transcendentals=exps)


SMEM = pl.BlockSpec(memory_space=pltpu.SMEM)
VMEM = pl.BlockSpec(memory_space=pltpu.VMEM)


def shape(*dims, dtype=BF):
    return jax.ShapeDtypeStruct(dims, dtype)


def stem_kernel(starts, place, sw_ref, pair_ref, other_ref, *rest):
    outs, ext = rest[:-1], rest[-1]
    n_rows, d0 = sw_ref.shape
    share = d0 // (len(FIRST) + len(SECOND))
    to = lax.broadcasted_iota(jnp.int32, (n_rows, n_rows), 0)
    of = lax.broadcasted_iota(jnp.int32, (n_rows, n_rows), 1)
    patch = n_rows // 4
    rows = jnp.where(of == (to % patch) * 4 + to // patch, 1.0, 0.0).astype(BF)
    sw = dot(rows, sw_ref[...]).astype(BF)
    at = 0
    ordered = []
    for group in (FIRST, SECOND):
        n = share * len(group)
        lane = lax.broadcasted_iota(jnp.int32, (1, n), 1)
        wanted = jnp.zeros((1, n), jnp.int32)
        for i in range(len(group)):
            here = (lane >= i * share) & (lane < (i + 1) * share)
            wanted = jnp.where(here, starts[at + i] + lane - i * share, wanted)
        chan = lax.broadcasted_iota(jnp.int32, (d0, n), 0)
        ordered.append(dot(sw, jnp.where(chan == wanted, 1.0, 0.0).astype(BF)).astype(BF))
        at += len(group)
    part = pair_ref.shape[0] // 2
    n_pos = part - 16
    y, zh, c = place[0], place[1], place[2]
    edge = jnp.full((STEP, ext.shape[1]), -1.0, F32)
    first = last = edge
    for i in range(4):
        ref = (pair_ref, other_ref)[i // 2]
        came = ref[i % 2 * part + n_pos : (i % 2 + 1) * part, :].astype(F32)
        first = jnp.where((y > 0) & (2 * (1 - c) + 1 - zh == i), came[16 - STEP :], first)
        last = jnp.where((y < NY - 1) & (2 * c + zh == i), came[:STEP], last)
    ext[0:8, :] = jnp.concatenate([edge, first])
    ext[8 + 4 * n_pos :, :] = jnp.concatenate([last, edge])
    blocks = [zh * 2 + c, (1 - zh) * 2 + c, zh * 2 + 1 - c, (1 - zh) * 2 + 1 - c]
    for i, b in enumerate(blocks):
        ref = (pair_ref, other_ref)[i // 2]
        block = ref[i % 2 * part : i % 2 * part + n_pos, :]
        ext[pl.ds(pl.multiple_of(8 + b * n_pos, 8), n_pos), :] = block.astype(F32)
    n = n_pos + 16
    for i, b in enumerate(blocks[2:] + blocks[:2]):
        ids = ext[pl.ds(pl.multiple_of(b * n_pos, 8), n), :]
        onehot = jnp.concatenate(
            [jnp.where(ids == k, 1.0, 0.0).astype(BF) for k in range(4)], axis=1
        )
        for g, weight in enumerate(ordered):
            stem = jax.nn.gelu(dot(onehot, weight))
            for t in range(3):
                at = STEP * (t + 1)
                outs[g * 3 + t][i * n_pos : (i + 1) * n_pos, :] = stem[at : at + n_pos].astype(BF)


def tap_weights(pieces, t):
    share = pieces[0].shape[0] // 3
    return jnp.concatenate([p[t * share : (t + 1) * share] for p in pieces])


def pack_kernel(sel, a1, a2, a3, out):
    n, half = a1.shape[0], out.shape[1]
    other = pl.ds(pl.multiple_of((1 - sel[0]) * half, half), half)
    out[:n, :] = a2[:, :half]
    out[n : 2 * n, :] = a2[:, half:]
    out[2 * n : 3 * n, :] = a1[:, other]
    out[3 * n :, :] = a3[:, other]


def pack(c, a1, a2, a3):
    rows, width = a1.shape
    return pl.pallas_call(
        pack_kernel,
        in_specs=[SMEM] + [VMEM] * 3,
        out_shape=shape(4 * rows, width // 2),
        compiler_params=params(),
        cost_estimate=cost(0),
    )(c, a1, a2, a3)


def pick_kernel(flip, sel, *refs):
    ins, out = refs[:-1], refs[-1]
    n = out.shape[0] // len(ins)
    k = 1 - sel[0] if flip else sel[0]
    for i, ref in enumerate(ins):
        out[i * n : (i + 1) * n, :] = ref[pl.ds(pl.multiple_of(k * n, 16), n), :]


def pick(c, arrays, n, flip):
    return pl.pallas_call(
        functools.partial(pick_kernel, flip),
        in_specs=[SMEM] + [VMEM] * len(arrays),
        out_shape=shape(n * len(arrays), arrays[0].shape[1]),
        compiler_params=params(),
        cost_estimate=cost(0),
    )(c, *arrays)


def conv1_kernel(sel, x0, x1, x2, own, a1, a2, a3, r, out):
    n, half = own.shape[0], out.shape[1]
    mine = pl.ds(pl.multiple_of(sel[0] * half, half), half)
    pieces = [own[:, mine], a1[:, mine], a3[:, mine], a2[:, mine]]
    pieces += [r[2 * n : 3 * n, :], r[3 * n :, :], r[pl.ds(pl.multiple_of(sel[0] * n, 16), n), :]]
    step = x0.shape[0] // 4

    def body(i, _):
        here = pl.ds(pl.multiple_of(i * step, step), step)
        total = None
        for t, x in enumerate((x0, x1, x2)):
            part = dot(x[here, :], tap_weights(pieces, t))
            total = part if total is None else total + part
        out[here, :] = total
        return 0

    lax.fori_loop(0, 4, body, 0)


def conv2_kernel(part, sel, acc, x0, x1, x2, b1, b3, swapped, last, out):
    n = last.shape[0]
    mine = pl.ds(pl.multiple_of(sel[0] * n, 16), n)
    pieces = []
    for b in (b1, b3):
        pieces += [b[mine, :], b[2 * n : 3 * n, :], b[3 * n :, :]]
    pieces += [swapped[:n, :], swapped[n:, :], last[...]]
    rows = out.shape[0] // 2
    for i in range(2):
        here = pl.ds((2 * part + i) * rows, rows)
        total = acc[here, :]
        for t, x in enumerate((x0, x1, x2)):
            total = total + dot(x[here, :], tap_weights(pieces, t))
        out[i * rows : (i + 1) * rows, :] = jax.nn.gelu(total).astype(BF)


def conv1(c, xs, pieces):
    rows, cols = xs[0].shape[0], pieces[0].shape[1] // 2
    return pl.pallas_call(
        conv1_kernel,
        in_specs=[SMEM] + [VMEM] * 8,
        out_shape=shape(rows, cols, dtype=F32),
        compiler_params=params(),
        cost_estimate=cost(6 * rows * xs[0].shape[1] * cols, 7 << 20),
    )(c, *xs, *pieces)


def conv2(c, acc, xs, pieces, part):
    rows, cols = acc.shape
    return pl.pallas_call(
        functools.partial(conv2_kernel, part),
        in_specs=[SMEM] + [VMEM] * 8,
        out_shape=shape(rows // 2, cols),
        compiler_params=params(),
        cost_estimate=cost(3 * rows * xs[0].shape[1] * cols, 4 << 20),
    )(c, acc, *xs, *pieces)


def project_kernel(sel, fk, fr, wq, wk, wv, q_mine, q_send, kv_out):
    n_pos, half, qc = fk.shape[0] // 2, fk.shape[1], wq.shape[1] // 2
    c = sel[0]
    my, other = [pl.ds(pl.multiple_of(k * half, half), half) for k in (c, 1 - c)]
    mine, theirs = [pl.ds(pl.multiple_of(k * qc, qc), qc) for k in (c, 1 - c)]
    wide_k, wide_r = fk[...].astype(F32), fr[...].astype(F32)
    squares = jnp.sum(wide_k * wide_k, -1, keepdims=True)
    squares = squares + jnp.sum(wide_r * wide_r, -1, keepdims=True)
    scale = lax.rsqrt(squares / (2 * half) + 1e-06)
    nk, nr = (wide_k * scale).astype(BF), (wide_r * scale).astype(BF)
    factor = HQK ** (-0.5) * math.log2(math.e)
    hk, hr = nk[:n_pos], nr[:n_pos]
    q_send[...] = ((dot(hk, wq[my, theirs]) + dot(hr, wq[other, theirs])) * factor).astype(BF)
    q_mine[...] = ((dot(hk, wq[my, mine]) + dot(hr, wq[other, mine])) * factor).astype(BF)
    n = 2 * n_pos
    kv_out[:n, :] = (dot(nk, wk[my, :]) + dot(nr, wk[other, :])).astype(BF)
    v = dot_t(nk, wv[:, my]) + dot_t(nr, wv[:, other])
    kv_out[n : 2 * n, :] = v[:, :128].astype(BF)
    tail = v[:, 128:]
    kv_out[2 * n :, :] = jnp.concatenate([tail[:n_pos], tail[n_pos:]], axis=1).astype(BF)


def project(c, f_keep, f_recv, query_weight, key_weight, value_weight):
    n, half = f_keep.shape
    n_pos = n // 2
    qc = query_weight.shape[1] // 2
    return pl.pallas_call(
        project_kernel,
        in_specs=[SMEM] + [VMEM] * 5,
        out_shape=[shape(n_pos, qc), shape(n_pos, qc), shape(5 * n_pos, 128)],
        compiler_params=params(),
        cost_estimate=cost(4 * n * half * 640, 4 << 20),
    )(c, f_keep, f_recv, query_weight, key_weight, value_weight)


def unpack(packed):
    n = packed.shape[0] // 5
    k, va, tail = packed[: 2 * n], packed[2 * n : 4 * n], packed[4 * n :]
    tail = tail.astype(F32)
    tail = jnp.concatenate([tail, pltpu.roll(tail, 64, 1)])
    lane = lax.broadcasted_iota(jnp.int32, tail.shape, 1)
    tail = jnp.where(lane < HV - 128, tail, jnp.where(lane == HV - 128, 1.0, 0.0))
    return k, jnp.concatenate([va, tail.astype(BF)], axis=1)


def attend_kernel(groups, first, last, *refs):
    qs = refs[:2]
    at = 2
    kvs = []
    for n in groups:
        kvs.append(unpack(jnp.concatenate([r[...] for r in refs[at : at + n]])))
        at += n
    rest = refs[at:]
    if not first:
        m_in, acc_in = rest[:2]
        rest = rest[2:]
    rows = qs[0].shape[0]
    for w in range(2):
        for h in range(HEADS // 2):
            q = qs[w][:, h * HQK : (h + 1) * HQK]
            scores = [dot_t(q, k) for k, _ in kvs]
            top = functools.reduce(
                jnp.maximum, [jnp.max(s, axis=1, keepdims=True) for s in scores]
            )
            here = pl.ds((w * 2 + h) * rows, rows)
            if not first:
                before = m_in[here, :1]
                top = jnp.maximum(top, before)
            total = None
            for s, (_, v) in zip(scores, kvs):
                part = dot(jnp.exp2(s - top).astype(BF), v)
                total = part if total is None else total + part
            if not first:
                total = total + acc_in[here, :] * jnp.exp2(before - top)
            if last:
                norm = total[:, :HV] / total[:, HV : HV + 1]
                rest[0][w * rows : (w + 1) * rows, h * HV : (h + 1) * HV] = norm.astype(BF)
            else:
                rest[0][here, :] = jnp.broadcast_to(top, (rows, 128))
                rest[1][here, :] = total


def attend(qs, kvs, state, last):
    rows = qs[0].shape[0]
    if last:
        out = shape(2 * rows, HEADS // 2 * HV)
    else:
        out = (shape(4 * rows, 128, dtype=F32), shape(4 * rows, 256, dtype=F32))
    n = sum(kv.shape[0] for group in kvs for kv in group) * 2 // 5
    return pl.pallas_call(
        functools.partial(attend_kernel, tuple(len(g) for g in kvs), not state, last),
        out_shape=out,
        compiler_params=params(),
        cost_estimate=cost(0),
    )(*qs, *[kv for group in kvs for kv in group], *state)


def finish_kernel(sel, fk, fr, attn, theirs, w, out):
    n_pos, cols = theirs.shape
    half = fk.shape[1]
    c = sel[0]
    mine, other = [pl.ds(pl.multiple_of(k * cols, cols), cols) for k in (c, 1 - c)]
    a, b = attn[:n_pos, :], theirs[...]
    ours, far = fk[:n_pos, :].astype(F32), fr[:n_pos, :].astype(F32)
    for k in range(2):
        rows = slice(k * half, (k + 1) * half)
        total = jnp.where(c == k, ours, far) + dot_t(a, w[rows, mine]) + dot_t(b, w[rows, other])
        out[:, rows] = total.astype(BF)


def finish(c, f_keep, f_recv, attn, theirs, out_weight):
    n_pos, cols = theirs.shape
    width = out_weight.shape[0]
    return pl.pallas_call(
        finish_kernel,
        in_specs=[SMEM] + [VMEM] * 5,
        out_shape=shape(n_pos, width),
        compiler_params=params(),
        cost_estimate=cost(4 * n_pos * width * cols, 4 << 20),
    )(c, f_keep, f_recv, attn, theirs, out_weight)


def grad_kernel(at, cot, cot_far, attn, own, one, two, three, total):
    n_pos, block = cot.shape[0], cot.shape[1] // 4
    a, b = attn[:n_pos, :], attn[n_pos:, :]
    down = lambda u, v: lax.dot_general(u, v, (((0,), (0,)), ((), ())), preferred_element_type=F32)
    for k in range(4):
        here = slice(k * block, (k + 1) * block)
        total[here, :] = down(cot[:, here], a) + down(cot_far[:, here], b)
    n = block // 16
    for k, out in enumerate((own, one, two, three)):
        x, y = (at[0] + k) % 4, (at[1] + k) % 4
        for i in range(16):
            start = jnp.where(at[2] == 0, x * block + i * n, i * 4 * n + y * n)
            rows = pl.ds(pl.multiple_of(start, 8), n)
            out[i * n : (i + 1) * n, :] = total[rows, :].astype(out.dtype)


def quarters(rows, cols):
    return [shape(rows, cols, dtype=F32)] + [shape(rows, cols)] * 3


def gradient(at, cot, cot_far, attn):
    block, cols = cot.shape[1] // 4, attn.shape[1]
    return pl.pallas_call(
        grad_kernel,
        in_specs=[SMEM] + [VMEM] * 3,
        out_shape=quarters(block, cols),
        scratch_shapes=[pltpu.VMEM((cot.shape[1], cols), F32)],
        compiler_params=params(),
        cost_estimate=cost(16 * cot.shape[0] * block * cols, 3 << 20),
    )(at, cot, cot_far, attn)


def again_kernel(at, own, a, b, d, mine, one, two, three, total):
    total[...] = own[...] + a[...].astype(F32) + b[...].astype(F32) + d[...].astype(F32)
    n = mine.shape[0] // 4
    for k, out in enumerate((mine, one, two, three)):
        x, y = (at[0] + k) % 4, (at[1] + k) % 4
        for zl in range(4):
            start = jnp.where(at[2] == 0, zl * 4 + y, x * 4 + zl) * n
            rows = pl.ds(pl.multiple_of(start, 8), n)
            out[zl * n : (zl + 1) * n, :] = total[rows, :].astype(out.dtype)


def again(at, own, came):
    rows, cols = own.shape
    return pl.pallas_call(
        again_kernel,
        in_specs=[SMEM] + [VMEM] * 4,
        out_shape=quarters(rows // 4, cols),
        scratch_shapes=[pltpu.VMEM((rows, cols), F32)],
        compiler_params=params(),
        cost_estimate=cost(rows * cols * 4),
    )(at, own, *came)


def split_z_kernel(own, a, b, d, out):
    total = own[...] + a[...].astype(F32) + b[...].astype(F32) + d[...].astype(F32)
    n = out.shape[1]
    for zl in range(4):
        for zh in range(2):
            at = (zl * 2 + zh) * n
            out[zh * 4 + zl] = total[at : at + n].astype(BF)


def split_z(own, came):
    rows, cols = own.shape
    return pl.pallas_call(
        split_z_kernel,
        in_specs=[VMEM] * 4,
        out_shape=shape(8, rows // 8, cols),
        compiler_params=params(),
        cost_estimate=cost(rows * cols * 4),
    )(own, *came)


def gather_kernel(sel, came, keep, away):
    total = jnp.sum(came[...].astype(F32), axis=0)
    n = total.shape[0] // 2
    keep[...] = jnp.where(sel[0] == 0, total[:n], total[n:])
    away[...] = jnp.where(sel[0] == 0, total[n:], total[:n])


def gathered(c, came):
    _, rows, cols = came.shape
    return pl.pallas_call(
        gather_kernel,
        in_specs=[SMEM, VMEM],
        out_shape=[shape(rows // 2, cols, dtype=F32)] * 2,
        compiler_params=params(),
        cost_estimate=cost(rows * cols * 32),
    )(c, came)


def local(
    dna_ids,
    stem_weight,
    kernel_taps_weight,
    query_weight,
    key_weight,
    value_weight,
    out_weight,
    cotangent,
):
    patch = stem_weight.shape[0] // 4
    n_pos = dna_ids.shape[1] // patch
    share, width = kernel_taps_weight.shape[1:]
    dp, seq = lax.axis_index("dp"), lax.axis_index("seq")
    x, zl = dp // 4, dp % 4
    y, zh, c = seq // 4, (seq // 2) % 2, seq % 2
    core = c.astype(jnp.int32).reshape(1)
    cat = lambda *a: jnp.concatenate(a)

    own = kernel_taps_weight.reshape(3 * share, width)
    a1, a3, a2 = [cores(own, "x", "z", k) for k in (1, -1, 2)]

    ids = lax.optimization_barrier(dna_ids.reshape(n_pos, patch).astype(BF))
    end = jnp.where(c == 1, ids[-16:], ids[:16])
    ids = cat(ids, round_ring(end, -1))
    far = send(ids, dz=4)

    starts = jnp.stack(
        [
            ((x + jnp.where(c == 0, i, j)) % 4 * 4 + (zl + jnp.where(c == 0, j, i)) % 4) * share
            for i, j in FIRST + SECOND
        ]
    ).astype(jnp.int32)
    n1, n2 = share * len(FIRST), share * len(SECOND)
    far, a1, a2, a3 = lax.optimization_barrier((far, a1, a2, a3))
    pair = cat(ids, far)
    other = send(pair, dc=1)
    xs = pl.pallas_call(
        stem_kernel,
        in_specs=[SMEM] * 2 + [VMEM] * 3,
        out_shape=[shape(4 * n_pos, n1)] * 3 + [shape(4 * n_pos, n2)] * 3,
        scratch_shapes=[pltpu.VMEM((4 * n_pos + 16, patch), F32)],
        compiler_params=params(),
        cost_estimate=cost(4 * 10**9, 8 << 20),
    )(starts, jnp.stack([y, zh, c]).astype(jnp.int32), stem_weight, pair, other)

    r = send(pack(core, a1, a2, a3), dc=1)
    b1, b3 = cores(r, "x", "z", 1), cores(r, "x", "z", -1)
    last = cores(pick(core, [r], 3 * share, False), "x", "z", 2)
    cot = cotangent[0]
    cot_far = send(cot, dc=1)

    acc = conv1(core, xs[:3], [own, a1, a2, a3, r])
    b1, b3, last, acc = lax.optimization_barrier((b1, b3, last, acc))
    pieces = [b1, b3, send(pick(core, [b1, b3], 3 * share, True), dc=1), last]
    f_recv = send(conv2(core, acc, xs[3:], pieces, 0), dc=1)
    f_keep = conv2(core, acc, xs[3:], pieces, 1)
    q_mine, q_send, kv = project(core, f_keep, f_recv, query_weight, key_weight, value_weight.T)

    r1 = round_ring(kv)
    qs = [q_mine, send(q_send, dc=1)]
    kv_o = send(kv, dc=1)
    r2 = round_ring(kv_o)
    state = attend(qs, [[kv], [kv_o]], (), False)
    r1, *state = lax.optimization_barrier((r1, *state))
    rr = round_ring(r1)
    r1_o, r2_o = send(r1, dc=1), send(r2, dc=1)
    state = attend(qs, [[r1], [r2], [r1_o], [r2_o]], state, False)
    rr, *state = lax.optimization_barrier((rr, *state))
    attn = attend(qs, [[rr], [send(rr, dc=1)]], state, True)

    at = jnp.stack([x, y, c]).astype(jnp.int32)
    own_part, *parts = gradient(at, cot, cot_far, attn)
    came = [cores(parts[k - 1], "x", "y", k) for k in (2, 1, 3)]
    attn, *_ = lax.optimization_barrier((attn, parts[0]))
    theirs = send(attn[n_pos:], dc=1)
    layer_out = finish(core, f_keep, f_recv, attn, theirs, out_weight)
    layer_out, *came = lax.optimization_barrier((layer_out, *came))
    own_part, *parts = again(at, own_part, came)
    came = [cores(parts[k - 1], "y", "x", k) for k in (2, 1, 3)]
    chunks = split_z(own_part, came)
    groups = [
        [flat(i, j, k, m) for k in range(NZ)]
        for i in range(NX)
        for j in range(NY)
        for m in range(2)
    ]
    came = lax.all_to_all(chunks, ("dp", "seq"), 0, 0, axis_index_groups=groups)
    keep, away = gathered(core, came)
    away = send(away, dc=1)
    out_grad = jnp.where(
        c == 0,
        jnp.concatenate([keep, away], axis=1),
        jnp.concatenate([away, keep], axis=1),
    )
    return (layer_out[None], out_grad)


def solution(mesh):
    placed = (P("dp", "seq"), P(), P(None, "dp", None), P(), P(), P(), P(), P("dp", "seq", None))
    return jax.shard_map(
        local,
        mesh=mesh,
        in_specs=placed,
        out_specs=(P("dp", "seq", None), P(("dp", "seq"), None)),
        check_vma=False,
    )
```

```python
import functools
import math

import jax
import jax.numpy as jnp
from jax import lax
from jax.experimental import pallas as pl
from jax.experimental.pallas import tpu as pltpu
from jax.sharding import PartitionSpec as P

HEADS = 4
HQK = 128
HV = 192
STEP = 4
NX, NY, NZ = 4, 4, 8
BF = jnp.bfloat16
F32 = jnp.float32

FIRST = ((0, 0), (3, 0), (1, 0), (2, 0), (0, 3), (0, 1), (0, 2))
SECOND = ((3, 2), (3, 3), (3, 1), (1, 2), (1, 3), (1, 1), (2, 3), (2, 1), (2, 2))


def flat(x, y, z, c):
    return (x * 4 + z % 4) * 16 + y * 4 + (z // 4) * 2 + c


def route(value, target):
    places = [(x, y, z, c) for x in range(NX) for y in range(NY) for z in range(NZ) for c in range(2)]
    pairs = [(flat(*p), flat(*target(*p))) for p in places if target(*p)]
    return lax.ppermute(value, ("dp", "seq"), pairs)


def send(value, dx=0, dy=0, dz=0, dc=0):
    return route(
        value, lambda x, y, z, c: ((x + dx) % NX, (y + dy) % NY, (z + dz) % NZ, c ^ dc)
    )


def cores(value, first, second, by):
    def target(x, y, z, c):
        to = {"x": x, "y": y, "z": z}
        axis = (first, second)[c]
        step = -by if axis == "z" and by == 2 and z % 2 else by
        to[axis] = (to[axis] + step) % {"x": NX, "y": NY, "z": NZ}[axis]
        return to["x"], to["y"], to["z"], c

    return route(value, target)


def round_ring(value, up=1):
    return route(value, lambda x, y, z, c: (x, (y + up * (1 - 2 * c)) % NY, z, c))


def dot(a, b):
    return jnp.dot(a, b, preferred_element_type=F32)


def dot_t(a, b):
    return lax.dot_general(a, b, (((1,), (1,)), ((), ())), preferred_element_type=F32)


def params():
    return pltpu.CompilerParams(vmem_limit_bytes=20 << 20)


def cost(flops, moved=1 << 20, exps=0):
    return pl.CostEstimate(flops=flops, bytes_accessed=moved, transcendentals=exps)


SMEM = pl.BlockSpec(memory_space=pltpu.SMEM)
VMEM = pl.BlockSpec(memory_space=pltpu.VMEM)


def shape(*dims, dtype=BF):
    return jax.ShapeDtypeStruct(dims, dtype)


def stem_kernel(place, sw_ref, ids_ref, far_ref, other_ref, far_other_ref, *rest):
    outs, ext = rest[:-1], rest[-1]
    refs = (ids_ref, far_ref, other_ref, far_other_ref)
    x, z_lo, y, zh, c = [place[i] for i in range(5)]
    n_rows, d0 = sw_ref.shape
    share = d0 // (len(FIRST) + len(SECOND))
    to = lax.broadcasted_iota(jnp.int32, (n_rows, n_rows), 0)
    of = lax.broadcasted_iota(jnp.int32, (n_rows, n_rows), 1)
    patch = n_rows // 4
    rows = jnp.where(of == (to % patch) * 4 + to // patch, 1.0, 0.0).astype(BF)
    sw = dot(rows, sw_ref[...]).astype(BF)
    ordered = []
    for group in (FIRST, SECOND):
        n = share * len(group)
        lane = lax.broadcasted_iota(jnp.int32, (1, n), 1)
        wanted = jnp.zeros((1, n), jnp.int32)
        for i, (near, across) in enumerate(group):
            ox, oz = jnp.where(c == 0, near, across), jnp.where(c == 0, across, near)
            start = ((x + ox) % 4 * 4 + (z_lo + oz) % 4) * share
            here = (lane >= i * share) & (lane < (i + 1) * share)
            wanted = jnp.where(here, start + lane - i * share, wanted)
        chan = lax.broadcasted_iota(jnp.int32, (d0, n), 0)
        ordered.append(dot(sw, jnp.where(chan == wanted, 1.0, 0.0).astype(BF)).astype(BF))
    n_pos = refs[0].shape[0] - 16
    edge = jnp.full((STEP, ext.shape[1]), -1.0, F32)
    first = last = edge
    for i in range(4):
        came = refs[i][n_pos:, :].astype(F32)
        first = jnp.where((y > 0) & (2 * (1 - c) + 1 - zh == i), came[16 - STEP :], first)
        last = jnp.where((y < NY - 1) & (2 * c + zh == i), came[:STEP], last)
    ext[0:8, :] = jnp.concatenate([edge, first])
    ext[8 + 4 * n_pos :, :] = jnp.concatenate([last, edge])
    blocks = [zh * 2 + c, (1 - zh) * 2 + c, zh * 2 + 1 - c, (1 - zh) * 2 + 1 - c]
    for i, b in enumerate(blocks):
        block = refs[i][:n_pos, :]
        ext[pl.ds(pl.multiple_of(8 + b * n_pos, 8), n_pos), :] = block.astype(F32)
    n = n_pos + 16
    for i, b in enumerate(blocks[2:] + blocks[:2]):
        ids = ext[pl.ds(pl.multiple_of(b * n_pos, 8), n), :]
        onehot = jnp.concatenate(
            [jnp.where(ids == k, 1.0, 0.0).astype(BF) for k in range(4)], axis=1
        )
        for g, weight in enumerate(ordered):
            stem = jax.nn.gelu(dot(onehot, weight))
            for t in range(3):
                at = STEP * (t + 1)
                outs[g * 3 + t][i * n_pos : (i + 1) * n_pos, :] = stem[at : at + n_pos].astype(BF)


def tap_weights(pieces, t):
    share = pieces[0].shape[0] // 3
    return jnp.concatenate([p[t * share : (t + 1) * share] for p in pieces])


def pack_kernel(sel, a1, a2, a3, out):
    n, half = a1.shape[0], out.shape[1]
    other = pl.ds(pl.multiple_of((1 - sel[0]) * half, half), half)
    out[:n, :] = a2[:, :half]
    out[n : 2 * n, :] = a2[:, half:]
    out[2 * n : 3 * n, :] = a1[:, other]
    out[3 * n :, :] = a3[:, other]


def pack(c, a1, a2, a3):
    rows, width = a1.shape
    return pl.pallas_call(
        pack_kernel,
        in_specs=[SMEM] + [VMEM] * 3,
        out_shape=shape(4 * rows, width // 2),
        compiler_params=params(),
        cost_estimate=cost(0),
    )(c, a1, a2, a3)


def pick_kernel(flip, sel, *refs):
    ins, out = refs[:-1], refs[-1]
    n = out.shape[0] // len(ins)
    k = 1 - sel[0] if flip else sel[0]
    for i, ref in enumerate(ins):
        out[i * n : (i + 1) * n, :] = ref[pl.ds(pl.multiple_of(k * n, 16), n), :]


def pick(c, arrays, n, flip):
    return pl.pallas_call(
        functools.partial(pick_kernel, flip),
        in_specs=[SMEM] + [VMEM] * len(arrays),
        out_shape=shape(n * len(arrays), arrays[0].shape[1]),
        compiler_params=params(),
        cost_estimate=cost(0),
    )(c, *arrays)


def conv1_kernel(sel, x0, x1, x2, own, a1, a2, a3, r, out):
    n, half = own.shape[0], out.shape[1]
    mine = pl.ds(pl.multiple_of(sel[0] * half, half), half)
    pieces = [own[:, mine], a1[:, mine], a3[:, mine], a2[:, mine]]
    pieces += [r[2 * n : 3 * n, :], r[3 * n :, :], r[pl.ds(pl.multiple_of(sel[0] * n, 16), n), :]]
    step = x0.shape[0] // 4

    def body(i, _):
        here = pl.ds(pl.multiple_of(i * step, step), step)
        total = None
        for t, x in enumerate((x0, x1, x2)):
            part = dot(x[here, :], tap_weights(pieces, t))
            total = part if total is None else total + part
        out[here, :] = total
        return 0

    lax.fori_loop(0, 4, body, 0)


def conv2_kernel(part, sel, acc, x0, x1, x2, b1, b3, swapped, last, out):
    n = last.shape[0]
    mine = pl.ds(pl.multiple_of(sel[0] * n, 16), n)
    pieces = []
    for b in (b1, b3):
        pieces += [b[mine, :], b[2 * n : 3 * n, :], b[3 * n :, :]]
    pieces += [swapped[:n, :], swapped[n:, :], last[...]]
    rows = out.shape[0] // 2
    for i in range(2):
        here = pl.ds((2 * part + i) * rows, rows)
        total = acc[here, :]
        for t, x in enumerate((x0, x1, x2)):
            total = total + dot(x[here, :], tap_weights(pieces, t))
        out[i * rows : (i + 1) * rows, :] = jax.nn.gelu(total).astype(BF)


def conv1(c, xs, pieces):
    rows, cols = xs[0].shape[0], pieces[0].shape[1] // 2
    return pl.pallas_call(
        conv1_kernel,
        in_specs=[SMEM] + [VMEM] * 8,
        out_shape=shape(rows, cols, dtype=F32),
        compiler_params=params(),
        cost_estimate=cost(6 * rows * xs[0].shape[1] * cols, 7 << 20),
    )(c, *xs, *pieces)


def conv2(c, acc, xs, pieces, part):
    rows, cols = acc.shape
    return pl.pallas_call(
        functools.partial(conv2_kernel, part),
        in_specs=[SMEM] + [VMEM] * 8,
        out_shape=shape(rows // 2, cols),
        compiler_params=params(),
        cost_estimate=cost(3 * rows * xs[0].shape[1] * cols, 4 << 20),
    )(c, acc, *xs, *pieces)


def project_kernel(sel, fk, fr, wq, wk, wv, q_mine, q_send, kv_out):
    n_pos, half, qc = fk.shape[0] // 2, fk.shape[1], wq.shape[1] // 2
    c = sel[0]
    my, other = [pl.ds(pl.multiple_of(k * half, half), half) for k in (c, 1 - c)]
    mine, theirs = [pl.ds(pl.multiple_of(k * qc, qc), qc) for k in (c, 1 - c)]
    wide_k, wide_r = fk[...].astype(F32), fr[...].astype(F32)
    squares = jnp.sum(wide_k * wide_k, -1, keepdims=True)
    squares = squares + jnp.sum(wide_r * wide_r, -1, keepdims=True)
    scale = lax.rsqrt(squares / (2 * half) + 1e-06)
    nk, nr = (wide_k * scale).astype(BF), (wide_r * scale).astype(BF)
    factor = HQK ** (-0.5) * math.log2(math.e)
    hk, hr = nk[:n_pos], nr[:n_pos]
    q_send[...] = ((dot(hk, wq[my, theirs]) + dot(hr, wq[other, theirs])) * factor).astype(BF)
    q_mine[...] = ((dot(hk, wq[my, mine]) + dot(hr, wq[other, mine])) * factor).astype(BF)
    n = 2 * n_pos
    kv_out[:n, :] = (dot(nk, wk[my, :]) + dot(nr, wk[other, :])).astype(BF)
    v = dot_t(nk, wv[:, my]) + dot_t(nr, wv[:, other])
    kv_out[n : 2 * n, :] = v[:, :128].astype(BF)
    tail = v[:, 128:]
    kv_out[2 * n :, :] = jnp.concatenate([tail[:n_pos], tail[n_pos:]], axis=1).astype(BF)


def project(c, f_keep, f_recv, query_weight, key_weight, value_weight):
    n, half = f_keep.shape
    n_pos = n // 2
    qc = query_weight.shape[1] // 2
    return pl.pallas_call(
        project_kernel,
        in_specs=[SMEM] + [VMEM] * 5,
        out_shape=[shape(n_pos, qc), shape(n_pos, qc), shape(5 * n_pos, 128)],
        compiler_params=params(),
        cost_estimate=cost(4 * n * half * 640, 4 << 20),
    )(c, f_keep, f_recv, query_weight, key_weight, value_weight)


def unpack(packed):
    n = packed.shape[0] // 5
    k, va, tail = packed[: 2 * n], packed[2 * n : 4 * n], packed[4 * n :]
    tail = tail.astype(F32)
    tail = jnp.concatenate([tail, pltpu.roll(tail, 64, 1)])
    lane = lax.broadcasted_iota(jnp.int32, tail.shape, 1)
    tail = jnp.where(lane < HV - 128, tail, jnp.where(lane == HV - 128, 1.0, 0.0))
    return k, jnp.concatenate([va, tail.astype(BF)], axis=1)


def attend_kernel(groups, first, last, *refs):
    qs = refs[:2]
    at = 2
    kvs = []
    for n in groups:
        kvs.append(unpack(jnp.concatenate([r[...] for r in refs[at : at + n]])))
        at += n
    rest = refs[at:]
    if not first:
        m_in, acc_in = rest[:2]
        rest = rest[2:]
    rows = qs[0].shape[0]
    for w in range(2):
        for h in range(HEADS // 2):
            q = qs[w][:, h * HQK : (h + 1) * HQK]
            scores = [dot_t(q, k) for k, _ in kvs]
            top = functools.reduce(
                jnp.maximum, [jnp.max(s, axis=1, keepdims=True) for s in scores]
            )
            here = pl.ds((w * 2 + h) * rows, rows)
            if not first:
                before = m_in[here, :1]
                top = jnp.maximum(top, before)
            total = None
            for s, (_, v) in zip(scores, kvs):
                part = dot(jnp.exp2(s - top).astype(BF), v)
                total = part if total is None else total + part
            if not first:
                total = total + acc_in[here, :] * jnp.exp2(before - top)
            if last:
                norm = total[:, :HV] / total[:, HV : HV + 1]
                rest[0][w * rows : (w + 1) * rows, h * HV : (h + 1) * HV] = norm.astype(BF)
            else:
                rest[0][here, :] = jnp.broadcast_to(top, (rows, 128))
                rest[1][here, :] = total


def attend(qs, kvs, state, last):
    rows = qs[0].shape[0]
    if last:
        out = shape(2 * rows, HEADS // 2 * HV)
    else:
        out = (shape(4 * rows, 128, dtype=F32), shape(4 * rows, 256, dtype=F32))
    n = sum(kv.shape[0] for group in kvs for kv in group) * 2 // 5
    return pl.pallas_call(
        functools.partial(attend_kernel, tuple(len(g) for g in kvs), not state, last),
        out_shape=out,
        compiler_params=params(),
        cost_estimate=cost(0),
    )(*qs, *[kv for group in kvs for kv in group], *state)


def finish_kernel(sel, fk, fr, attn, theirs, w, out):
    n_pos, cols = theirs.shape
    half = fk.shape[1]
    c = sel[0]
    mine, other = [pl.ds(pl.multiple_of(k * cols, cols), cols) for k in (c, 1 - c)]
    a, b = attn[:n_pos, :], theirs[...]
    ours, far = fk[:n_pos, :].astype(F32), fr[:n_pos, :].astype(F32)
    for k in range(2):
        rows = slice(k * half, (k + 1) * half)
        total = jnp.where(c == k, ours, far) + dot_t(a, w[rows, mine]) + dot_t(b, w[rows, other])
        out[:, rows] = total.astype(BF)


def finish(c, f_keep, f_recv, attn, theirs, out_weight):
    n_pos, cols = theirs.shape
    width = out_weight.shape[0]
    return pl.pallas_call(
        finish_kernel,
        in_specs=[SMEM] + [VMEM] * 5,
        out_shape=shape(n_pos, width),
        compiler_params=params(),
        cost_estimate=cost(4 * n_pos * width * cols, 4 << 20),
    )(c, f_keep, f_recv, attn, theirs, out_weight)


def grad_kernel(at, cot, cot_far, attn, own, one, two, three, total):
    n_pos, block = cot.shape[0], cot.shape[1] // 4
    a, b = attn[:n_pos, :], attn[n_pos:, :]
    down = lambda u, v: lax.dot_general(u, v, (((0,), (0,)), ((), ())), preferred_element_type=F32)
    for k in range(4):
        here = slice(k * block, (k + 1) * block)
        total[here, :] = down(cot[:, here], a) + down(cot_far[:, here], b)
    n = block // 16
    for k, out in enumerate((own, one, two, three)):
        x, y = (at[0] + k) % 4, (at[1] + k) % 4
        for i in range(16):
            start = jnp.where(at[2] == 0, x * block + i * n, i * 4 * n + y * n)
            rows = pl.ds(pl.multiple_of(start, 8), n)
            out[i * n : (i + 1) * n, :] = total[rows, :].astype(out.dtype)


def quarters(rows, cols):
    return [shape(rows, cols, dtype=F32)] + [shape(rows, cols)] * 3


def gradient(at, cot, cot_far, attn):
    block, cols = cot.shape[1] // 4, attn.shape[1]
    return pl.pallas_call(
        grad_kernel,
        in_specs=[SMEM] + [VMEM] * 3,
        out_shape=quarters(block, cols),
        scratch_shapes=[pltpu.VMEM((cot.shape[1], cols), F32)],
        compiler_params=params(),
        cost_estimate=cost(16 * cot.shape[0] * block * cols, 3 << 20),
    )(at, cot, cot_far, attn)


def again_kernel(at, own, a, b, d, mine, one, two, three, total):
    total[...] = own[...] + a[...].astype(F32) + b[...].astype(F32) + d[...].astype(F32)
    n = mine.shape[0] // 4
    for k, out in enumerate((mine, one, two, three)):
        x, y = (at[0] + k) % 4, (at[1] + k) % 4
        for zl in range(4):
            start = jnp.where(at[2] == 0, zl * 4 + y, x * 4 + zl) * n
            rows = pl.ds(pl.multiple_of(start, 8), n)
            out[zl * n : (zl + 1) * n, :] = total[rows, :].astype(out.dtype)


def again(at, own, came):
    rows, cols = own.shape
    return pl.pallas_call(
        again_kernel,
        in_specs=[SMEM] + [VMEM] * 4,
        out_shape=quarters(rows // 4, cols),
        scratch_shapes=[pltpu.VMEM((rows, cols), F32)],
        compiler_params=params(),
        cost_estimate=cost(rows * cols * 4),
    )(at, own, *came)


def split_z_kernel(own, a, b, d, out):
    total = own[...] + a[...].astype(F32) + b[...].astype(F32) + d[...].astype(F32)
    n = out.shape[1]
    for zl in range(4):
        for zh in range(2):
            at = (zl * 2 + zh) * n
            out[zh * 4 + zl] = total[at : at + n].astype(BF)


def split_z(own, came):
    rows, cols = own.shape
    return pl.pallas_call(
        split_z_kernel,
        in_specs=[VMEM] * 4,
        out_shape=shape(8, rows // 8, cols),
        compiler_params=params(),
        cost_estimate=cost(rows * cols * 4),
    )(own, *came)


def gather_kernel(sel, came, keep, away):
    total = jnp.sum(came[...].astype(F32), axis=0)
    n = total.shape[0] // 2
    keep[...] = jnp.where(sel[0] == 0, total[:n], total[n:])
    away[...] = jnp.where(sel[0] == 0, total[n:], total[:n])


def gathered(c, came):
    _, rows, cols = came.shape
    return pl.pallas_call(
        gather_kernel,
        in_specs=[SMEM, VMEM],
        out_shape=[shape(rows // 2, cols, dtype=F32)] * 2,
        compiler_params=params(),
        cost_estimate=cost(rows * cols * 32),
    )(c, came)


def join_kernel(sel, keep, away, out):
    cols = keep.shape[1]
    out[:, :cols] = jnp.where(sel[0] == 0, keep[...], away[...])
    out[:, cols:] = jnp.where(sel[0] == 0, away[...], keep[...])


def join(c, keep, away):
    rows, cols = keep.shape
    return pl.pallas_call(
        join_kernel,
        in_specs=[SMEM] + [VMEM] * 2,
        out_shape=shape(rows, 2 * cols, dtype=F32),
        compiler_params=params(),
        cost_estimate=cost(0),
    )(c, keep, away)


def local(
    dna_ids,
    stem_weight,
    kernel_taps_weight,
    query_weight,
    key_weight,
    value_weight,
    out_weight,
    cotangent,
):
    patch = stem_weight.shape[0] // 4
    n_pos = dna_ids.shape[1] // patch
    share, width = kernel_taps_weight.shape[1:]
    dp, seq = lax.axis_index("dp"), lax.axis_index("seq")
    x, zl = dp // 4, dp % 4
    y, zh, c = seq // 4, (seq // 2) % 2, seq % 2
    core = c.astype(jnp.int32).reshape(1)
    place = jnp.stack([x, zl, y, zh, c]).astype(jnp.int32)
    at = jnp.stack([x, y, c]).astype(jnp.int32)
    core, place, at, dna_ids = lax.optimization_barrier((core, place, at, dna_ids))
    cat = lambda *a: jnp.concatenate(a)

    own = kernel_taps_weight.reshape(3 * share, width)
    a1, a3, a2 = [cores(own, "x", "z", k) for k in (1, -1, 2)]

    ids = lax.optimization_barrier(dna_ids.reshape(n_pos, patch).astype(BF))
    end = jnp.where(c == 1, ids[-16:], ids[:16])
    ids = cat(ids, round_ring(end, -1))
    far, other = send(ids, dz=4), send(ids, dc=1)

    widths = [share * len(g) for g in (FIRST, SECOND)]
    far, other, a1, a2, a3 = lax.optimization_barrier((far, other, a1, a2, a3))
    far_other = send(far, dc=1)
    xs = pl.pallas_call(
        stem_kernel,
        in_specs=[SMEM] + [VMEM] * 5,
        out_shape=[shape(4 * n_pos, n) for n in widths for _ in range(3)],
        scratch_shapes=[pltpu.VMEM((4 * n_pos + 16, patch), F32)],
        compiler_params=params(),
        cost_estimate=cost(4 * 10**9, 8 << 20),
    )(place, stem_weight, ids, far, other, far_other)

    r = send(pack(core, a1, a2, a3), dc=1)
    b1, b3 = cores(r, "x", "z", 1), cores(r, "x", "z", -1)
    last = cores(pick(core, [r], 3 * share, False), "x", "z", 2)
    cot = cotangent[0]
    cot_far = send(cot, dc=1)

    acc = conv1(core, xs[:3], [own, a1, a2, a3, r])
    b1, b3, last, acc = lax.optimization_barrier((b1, b3, last, acc))
    pieces = [b1, b3, send(pick(core, [b1, b3], 3 * share, True), dc=1), last]
    f_recv = send(conv2(core, acc, xs[3:], pieces, 0), dc=1)
    f_keep = conv2(core, acc, xs[3:], pieces, 1)
    q_mine, q_send, kv = project(core, f_keep, f_recv, query_weight, key_weight, value_weight.T)

    r1, r2 = round_ring(kv), round_ring(kv, -1)
    qs = [q_mine, send(q_send, dc=1)]
    state = attend(qs, [[kv], [send(kv, dc=1)]], (), False)
    r1, r2, *state = lax.optimization_barrier((r1, r2, *state))
    rr = round_ring(r1)
    r1_o, r2_o = send(r1, dc=1), send(r2, dc=1)
    state = attend(qs, [[r1], [r2]], state, False)
    state = attend(qs, [[r1_o], [r2_o]], state, False)
    rr, *state = lax.optimization_barrier((rr, *state))
    attn = attend(qs, [[rr], [send(rr, dc=1)]], state, True)

    own_part, *parts = gradient(at, cot, cot_far, attn)
    came = [cores(parts[k - 1], "x", "y", k) for k in (2, 1, 3)]
    attn, *_ = lax.optimization_barrier((attn, parts[0]))
    theirs = send(attn[n_pos:], dc=1)
    layer_out = finish(core, f_keep, f_recv, attn, theirs, out_weight)
    layer_out, *came = lax.optimization_barrier((layer_out, *came))
    own_part, *parts = again(at, own_part, came)
    came = [cores(parts[k - 1], "y", "x", k) for k in (2, 1, 3)]
    chunks = split_z(own_part, came)
    groups = [
        [flat(i, j, k, m) for k in range(NZ)]
        for i in range(NX)
        for j in range(NY)
        for m in range(2)
    ]
    came = lax.all_to_all(chunks, ("dp", "seq"), 0, 0, axis_index_groups=groups)
    keep, away = gathered(core, came)
    away = send(away, dc=1)
    out_grad = join(core, keep, away)
    return (layer_out[None], out_grad)


def solution(mesh):
    placed = (P("dp", "seq"), P(), P(None, "dp", None), P(), P(), P(), P(), P("dp", "seq", None))
    return jax.shard_map(
        local,
        mesh=mesh,
        in_specs=placed,
        out_specs=(P("dp", "seq", None), P(("dp", "seq"), None)),
        check_vma=False,
    )
```

```python
import functools
import math

import jax
import jax.numpy as jnp
from jax import lax
from jax.experimental import pallas as pl
from jax.experimental.pallas import tpu as pltpu
from jax.sharding import PartitionSpec as P

HEADS = 4
HQK = 128
HV = 192
STEP = 4
NX, NY, NZ = 4, 4, 8
BF = jnp.bfloat16
F32 = jnp.float32

FIRST = ((0, 0), (3, 0), (1, 0), (2, 0), (0, 3), (0, 1), (0, 2))
SECOND = ((3, 2), (3, 3), (3, 1), (1, 2), (1, 3), (1, 1), (2, 3), (2, 1), (2, 2))


def flat(x, y, z, c):
    return (x * 4 + z % 4) * 16 + y * 4 + (z // 4) * 2 + c


def route(value, target):
    places = [(x, y, z, c) for x in range(NX) for y in range(NY) for z in range(NZ) for c in range(2)]
    pairs = [(flat(*p), flat(*target(*p))) for p in places if target(*p)]
    return lax.ppermute(value, ("dp", "seq"), pairs)


def send(value, dx=0, dy=0, dz=0, dc=0):
    return route(
        value, lambda x, y, z, c: ((x + dx) % NX, (y + dy) % NY, (z + dz) % NZ, c ^ dc)
    )


def cores(value, first, second, by):
    def target(x, y, z, c):
        to = {"x": x, "y": y, "z": z}
        axis = (first, second)[c]
        step = -by if axis == "z" and by == 2 and z % 2 else by
        to[axis] = (to[axis] + step) % {"x": NX, "y": NY, "z": NZ}[axis]
        return to["x"], to["y"], to["z"], c

    return route(value, target)


def round_ring(value, up=1):
    return route(value, lambda x, y, z, c: (x, (y + up * (1 - 2 * c)) % NY, z, c))


def dot(a, b):
    return jnp.dot(a, b, preferred_element_type=F32)


def dot_t(a, b):
    return lax.dot_general(a, b, (((1,), (1,)), ((), ())), preferred_element_type=F32)


def params():
    return pltpu.CompilerParams(vmem_limit_bytes=20 << 20)


def cost(flops, moved=1 << 20, exps=0):
    return pl.CostEstimate(flops=flops, bytes_accessed=moved, transcendentals=exps)


SMEM = pl.BlockSpec(memory_space=pltpu.SMEM)
VMEM = pl.BlockSpec(memory_space=pltpu.VMEM)


def shape(*dims, dtype=BF):
    return jax.ShapeDtypeStruct(dims, dtype)


def stem_kernel(place, sw_ref, ids_ref, far_ref, other_ref, far_other_ref, *rest):
    outs, ext = rest[:-1], rest[-1]
    refs = (ids_ref, far_ref, other_ref, far_other_ref)
    x, z_lo, y, zh, c = [place[i] for i in range(5)]
    n_rows, d0 = sw_ref.shape
    share = d0 // (len(FIRST) + len(SECOND))
    to = lax.broadcasted_iota(jnp.int32, (n_rows, n_rows), 0)
    of = lax.broadcasted_iota(jnp.int32, (n_rows, n_rows), 1)
    patch = n_rows // 4
    rows = jnp.where(of == (to % patch) * 4 + to // patch, 1.0, 0.0).astype(BF)
    sw = dot(rows, sw_ref[...]).astype(BF)
    ordered = []
    for group in (FIRST, SECOND):
        n = share * len(group)
        lane = lax.broadcasted_iota(jnp.int32, (1, n), 1)
        wanted = jnp.zeros((1, n), jnp.int32)
        for i, (near, across) in enumerate(group):
            ox, oz = jnp.where(c == 0, near, across), jnp.where(c == 0, across, near)
            start = ((x + ox) % 4 * 4 + (z_lo + oz) % 4) * share
            here = (lane >= i * share) & (lane < (i + 1) * share)
            wanted = jnp.where(here, start + lane - i * share, wanted)
        chan = lax.broadcasted_iota(jnp.int32, (d0, n), 0)
        ordered.append(dot(sw, jnp.where(chan == wanted, 1.0, 0.0).astype(BF)).astype(BF))
    n_pos = refs[0].shape[0] - 16
    edge = jnp.full((STEP, ext.shape[1]), -1.0, F32)
    first = last = edge
    for i in range(4):
        came = refs[i][n_pos:, :].astype(F32)
        first = jnp.where((y > 0) & (2 * (1 - c) + 1 - zh == i), came[16 - STEP :], first)
        last = jnp.where((y < NY - 1) & (2 * c + zh == i), came[:STEP], last)
    ext[0:8, :] = jnp.concatenate([edge, first])
    ext[8 + 4 * n_pos :, :] = jnp.concatenate([last, edge])
    blocks = [zh * 2 + c, (1 - zh) * 2 + c, zh * 2 + 1 - c, (1 - zh) * 2 + 1 - c]
    for i, b in enumerate(blocks):
        block = refs[i][:n_pos, :]
        ext[pl.ds(pl.multiple_of(8 + b * n_pos, 8), n_pos), :] = block.astype(F32)
    n = n_pos + 16
    for i, b in enumerate(blocks[2:] + blocks[:2]):
        ids = ext[pl.ds(pl.multiple_of(b * n_pos, 8), n), :]
        onehot = jnp.concatenate(
            [jnp.where(ids == k, 1.0, 0.0).astype(BF) for k in range(4)], axis=1
        )
        for g, weight in enumerate(ordered):
            stem = jax.nn.gelu(dot(onehot, weight))
            for t in range(3):
                at = STEP * (t + 1)
                outs[g * 3 + t][i * n_pos : (i + 1) * n_pos, :] = stem[at : at + n_pos].astype(BF)


def tap_weights(pieces, t):
    share = pieces[0].shape[0] // 3
    return jnp.concatenate([p[t * share : (t + 1) * share] for p in pieces])


def pack_kernel(sel, a1, a2, a3, out):
    n, half = a1.shape[0], out.shape[1]
    other = pl.ds(pl.multiple_of((1 - sel[0]) * half, half), half)
    out[:n, :] = a2[:, :half]
    out[n : 2 * n, :] = a2[:, half:]
    out[2 * n : 3 * n, :] = a1[:, other]
    out[3 * n :, :] = a3[:, other]


def pack(c, a1, a2, a3):
    rows, width = a1.shape
    return pl.pallas_call(
        pack_kernel,
        in_specs=[SMEM] + [VMEM] * 3,
        out_shape=shape(4 * rows, width // 2),
        compiler_params=params(),
        cost_estimate=cost(0),
    )(c, a1, a2, a3)


def pick_kernel(flip, sel, *refs):
    ins, out = refs[:-1], refs[-1]
    n = out.shape[0] // len(ins)
    k = 1 - sel[0] if flip else sel[0]
    for i, ref in enumerate(ins):
        out[i * n : (i + 1) * n, :] = ref[pl.ds(pl.multiple_of(k * n, 16), n), :]


def pick(c, arrays, n, flip):
    return pl.pallas_call(
        functools.partial(pick_kernel, flip),
        in_specs=[SMEM] + [VMEM] * len(arrays),
        out_shape=shape(n * len(arrays), arrays[0].shape[1]),
        compiler_params=params(),
        cost_estimate=cost(0),
    )(c, *arrays)


def conv1_kernel(sel, x0, x1, x2, own, a1, a2, a3, r, out):
    n, half = own.shape[0], out.shape[1]
    mine = pl.ds(pl.multiple_of(sel[0] * half, half), half)
    pieces = [own[:, mine], a1[:, mine], a3[:, mine], a2[:, mine]]
    pieces += [r[2 * n : 3 * n, :], r[3 * n :, :], r[pl.ds(pl.multiple_of(sel[0] * n, 16), n), :]]
    step = x0.shape[0] // 4

    def body(i, _):
        here = pl.ds(pl.multiple_of(i * step, step), step)
        total = None
        for t, x in enumerate((x0, x1, x2)):
            part = dot(x[here, :], tap_weights(pieces, t))
            total = part if total is None else total + part
        out[here, :] = total
        return 0

    lax.fori_loop(0, 4, body, 0)


def conv2_kernel(part, sel, acc, x0, x1, x2, b1, b3, swapped, last, out):
    n = last.shape[0]
    mine = pl.ds(pl.multiple_of(sel[0] * n, 16), n)
    pieces = []
    for b in (b1, b3):
        pieces += [b[mine, :], b[2 * n : 3 * n, :], b[3 * n :, :]]
    pieces += [swapped[:n, :], swapped[n:, :], last[...]]
    rows = out.shape[0] // 2
    for i in range(2):
        here = pl.ds((2 * part + i) * rows, rows)
        total = acc[here, :]
        for t, x in enumerate((x0, x1, x2)):
            total = total + dot(x[here, :], tap_weights(pieces, t))
        out[i * rows : (i + 1) * rows, :] = jax.nn.gelu(total).astype(BF)


def conv1(c, xs, pieces):
    rows, cols = xs[0].shape[0], pieces[0].shape[1] // 2
    return pl.pallas_call(
        conv1_kernel,
        in_specs=[SMEM] + [VMEM] * 8,
        out_shape=shape(rows, cols, dtype=F32),
        compiler_params=params(),
        cost_estimate=cost(6 * rows * xs[0].shape[1] * cols, 7 << 20),
    )(c, *xs, *pieces)


def conv2(c, acc, xs, pieces, part):
    rows, cols = acc.shape
    return pl.pallas_call(
        functools.partial(conv2_kernel, part),
        in_specs=[SMEM] + [VMEM] * 8,
        out_shape=shape(rows // 2, cols),
        compiler_params=params(),
        cost_estimate=cost(3 * rows * xs[0].shape[1] * cols, 4 << 20),
    )(c, acc, *xs, *pieces)


def project_kernel(sel, fk, fr, wq, wk, wv, q_mine, q_send, kv_out):
    n_pos, half, qc = fk.shape[0] // 2, fk.shape[1], wq.shape[1] // 2
    c = sel[0]
    my, other = [pl.ds(pl.multiple_of(k * half, half), half) for k in (c, 1 - c)]
    mine, theirs = [pl.ds(pl.multiple_of(k * qc, qc), qc) for k in (c, 1 - c)]
    wide_k, wide_r = fk[...].astype(F32), fr[...].astype(F32)
    squares = jnp.sum(wide_k * wide_k, -1, keepdims=True)
    squares = squares + jnp.sum(wide_r * wide_r, -1, keepdims=True)
    scale = lax.rsqrt(squares / (2 * half) + 1e-06)
    nk, nr = (wide_k * scale).astype(BF), (wide_r * scale).astype(BF)
    factor = HQK ** (-0.5) * math.log2(math.e)
    hk, hr = nk[:n_pos], nr[:n_pos]
    q_send[...] = ((dot(hk, wq[my, theirs]) + dot(hr, wq[other, theirs])) * factor).astype(BF)
    q_mine[...] = ((dot(hk, wq[my, mine]) + dot(hr, wq[other, mine])) * factor).astype(BF)
    n = 2 * n_pos
    kv_out[:n, :] = (dot(nk, wk[my, :]) + dot(nr, wk[other, :])).astype(BF)
    v = dot_t(nk, wv[:, my]) + dot_t(nr, wv[:, other])
    kv_out[n : 2 * n, :] = v[:, :128].astype(BF)
    tail = v[:, 128:]
    kv_out[2 * n :, :] = jnp.concatenate([tail[:n_pos], tail[n_pos:]], axis=1).astype(BF)


def project(c, f_keep, f_recv, query_weight, key_weight, value_weight):
    n, half = f_keep.shape
    n_pos = n // 2
    qc = query_weight.shape[1] // 2
    return pl.pallas_call(
        project_kernel,
        in_specs=[SMEM] + [VMEM] * 5,
        out_shape=[shape(n_pos, qc), shape(n_pos, qc), shape(5 * n_pos, 128)],
        compiler_params=params(),
        cost_estimate=cost(4 * n * half * 640, 4 << 20),
    )(c, f_keep, f_recv, query_weight, key_weight, value_weight)


def unpack(packed):
    n = packed.shape[0] // 5
    k, va, tail = packed[: 2 * n], packed[2 * n : 4 * n], packed[4 * n :]
    tail = tail.astype(F32)
    tail = jnp.concatenate([tail, pltpu.roll(tail, 64, 1)])
    lane = lax.broadcasted_iota(jnp.int32, tail.shape, 1)
    tail = jnp.where(lane < HV - 128, tail, jnp.where(lane == HV - 128, 1.0, 0.0))
    return k, jnp.concatenate([va, tail.astype(BF)], axis=1)


def attend_kernel(groups, first, last, *refs):
    qs = refs[:2]
    at = 2
    kvs = []
    for n in groups:
        kvs.append(unpack(jnp.concatenate([r[...] for r in refs[at : at + n]])))
        at += n
    rest = refs[at:]
    if not first:
        m_in, acc_in = rest[:2]
        rest = rest[2:]
    rows = qs[0].shape[0]
    for w in range(2):
        for h in range(HEADS // 2):
            q = qs[w][:, h * HQK : (h + 1) * HQK]
            scores = [dot_t(q, k) for k, _ in kvs]
            top = functools.reduce(
                jnp.maximum, [jnp.max(s, axis=1, keepdims=True) for s in scores]
            )
            here = pl.ds((w * 2 + h) * rows, rows)
            if not first:
                before = m_in[here, :1]
                top = jnp.maximum(top, before)
            total = None
            for s, (_, v) in zip(scores, kvs):
                part = dot(jnp.exp2(s - top).astype(BF), v)
                total = part if total is None else total + part
            if not first:
                total = total + acc_in[here, :] * jnp.exp2(before - top)
            if last:
                norm = total[:, :HV] / total[:, HV : HV + 1]
                rest[0][w * rows : (w + 1) * rows, h * HV : (h + 1) * HV] = norm.astype(BF)
            else:
                rest[0][here, :] = jnp.broadcast_to(top, (rows, 128))
                rest[1][here, :] = total


def attend(qs, kvs, state, last):
    rows = qs[0].shape[0]
    if last:
        out = shape(2 * rows, HEADS // 2 * HV)
    else:
        out = (shape(4 * rows, 128, dtype=F32), shape(4 * rows, 256, dtype=F32))
    n = sum(kv.shape[0] for group in kvs for kv in group) * 2 // 5
    return pl.pallas_call(
        functools.partial(attend_kernel, tuple(len(g) for g in kvs), not state, last),
        out_shape=out,
        compiler_params=params(),
        cost_estimate=cost(0),
    )(*qs, *[kv for group in kvs for kv in group], *state)


def finish_kernel(sel, fk, fr, attn, theirs, w, out):
    n_pos, cols = theirs.shape
    half = fk.shape[1]
    c = sel[0]
    mine, other = [pl.ds(pl.multiple_of(k * cols, cols), cols) for k in (c, 1 - c)]
    a, b = attn[:n_pos, :], theirs[...]
    ours, far = fk[:n_pos, :].astype(F32), fr[:n_pos, :].astype(F32)
    for k in range(2):
        rows = slice(k * half, (k + 1) * half)
        total = jnp.where(c == k, ours, far) + dot_t(a, w[rows, mine]) + dot_t(b, w[rows, other])
        out[:, rows] = total.astype(BF)


def finish(c, f_keep, f_recv, attn, theirs, out_weight):
    n_pos, cols = theirs.shape
    width = out_weight.shape[0]
    return pl.pallas_call(
        finish_kernel,
        in_specs=[SMEM] + [VMEM] * 5,
        out_shape=shape(n_pos, width),
        compiler_params=params(),
        cost_estimate=cost(4 * n_pos * width * cols, 4 << 20),
    )(c, f_keep, f_recv, attn, theirs, out_weight)


def grad_kernel(at, cot, cot_far, attn, own, one, two, three, total):
    n_pos, block = cot.shape[0], cot.shape[1] // 4
    a, b = attn[:n_pos, :], attn[n_pos:, :]
    down = lambda u, v: lax.dot_general(u, v, (((0,), (0,)), ((), ())), preferred_element_type=F32)
    for k in range(4):
        here = slice(k * block, (k + 1) * block)
        total[here, :] = down(cot[:, here], a) + down(cot_far[:, here], b)
    n = block // 16
    for k, out in enumerate((own, one, two, three)):
        x, y = (at[0] + k) % 4, (at[1] + k) % 4
        for i in range(16):
            start = jnp.where(at[2] == 0, x * block + i * n, i * 4 * n + y * n)
            rows = pl.ds(pl.multiple_of(start, 8), n)
            out[i * n : (i + 1) * n, :] = total[rows, :].astype(out.dtype)


def quarters(rows, cols):
    return [shape(rows, cols, dtype=F32)] + [shape(rows, cols)] * 3


def gradient(at, cot, cot_far, attn):
    block, cols = cot.shape[1] // 4, attn.shape[1]
    return pl.pallas_call(
        grad_kernel,
        in_specs=[SMEM] + [VMEM] * 3,
        out_shape=quarters(block, cols),
        scratch_shapes=[pltpu.VMEM((cot.shape[1], cols), F32)],
        compiler_params=params(),
        cost_estimate=cost(16 * cot.shape[0] * block * cols, 3 << 20),
    )(at, cot, cot_far, attn)


def chunks_kernel(at, own, a, b, d, out, total):
    total[...] = own[...] + a[...].astype(F32) + b[...].astype(F32) + d[...].astype(F32)
    n = out.shape[1]
    for j in range(4):
        for zl in range(4):
            start = jnp.where(at[2] == 0, zl * 4 + j, j * 4 + zl) * 2 * n
            rows = total[pl.ds(pl.multiple_of(start, 8), 2 * n), :].astype(BF)
            out[j * 8 + zl] = rows[:n]
            out[j * 8 + 4 + zl] = rows[n:]


def chunks_of(at, own, came):
    rows, cols = own.shape
    return pl.pallas_call(
        chunks_kernel,
        in_specs=[SMEM] + [VMEM] * 4,
        out_shape=shape(32, rows // 32, cols),
        scratch_shapes=[pltpu.VMEM((rows, cols), F32)],
        compiler_params=params(),
        cost_estimate=cost(rows * cols * 4),
    )(at, own, *came)


def gather_kernel(sel, came, keep, away):
    total = jnp.sum(came[...].astype(F32), axis=0)
    n = total.shape[0] // 2
    keep[...] = jnp.where(sel[0] == 0, total[:n], total[n:])
    away[...] = jnp.where(sel[0] == 0, total[n:], total[:n])


def gathered(c, came):
    _, rows, cols = came.shape
    return pl.pallas_call(
        gather_kernel,
        in_specs=[SMEM, VMEM],
        out_shape=[shape(rows // 2, cols, dtype=F32)] * 2,
        compiler_params=params(),
        cost_estimate=cost(rows * cols * 32),
    )(c, came)


def join_kernel(sel, keep, away, out):
    cols = keep.shape[1]
    out[:, :cols] = jnp.where(sel[0] == 0, keep[...], away[...])
    out[:, cols:] = jnp.where(sel[0] == 0, away[...], keep[...])


def join(c, keep, away):
    rows, cols = keep.shape
    return pl.pallas_call(
        join_kernel,
        in_specs=[SMEM] + [VMEM] * 2,
        out_shape=shape(rows, 2 * cols, dtype=F32),
        compiler_params=params(),
        cost_estimate=cost(0),
    )(c, keep, away)


def local(
    dna_ids,
    stem_weight,
    kernel_taps_weight,
    query_weight,
    key_weight,
    value_weight,
    out_weight,
    cotangent,
):
    patch = stem_weight.shape[0] // 4
    n_pos = dna_ids.shape[1] // patch
    share, width = kernel_taps_weight.shape[1:]
    dp, seq = lax.axis_index("dp"), lax.axis_index("seq")
    x, zl = dp // 4, dp % 4
    y, zh, c = seq // 4, (seq // 2) % 2, seq % 2
    core = c.astype(jnp.int32).reshape(1)
    place = jnp.stack([x, zl, y, zh, c]).astype(jnp.int32)
    at = jnp.stack([x, y, c]).astype(jnp.int32)
    core, place, at, dna_ids = lax.optimization_barrier((core, place, at, dna_ids))
    cat = lambda *a: jnp.concatenate(a)

    own = kernel_taps_weight.reshape(3 * share, width)
    a1, a3, a2 = [cores(own, "x", "z", k) for k in (1, -1, 2)]

    ids = lax.optimization_barrier(dna_ids.reshape(n_pos, patch).astype(BF))
    end = jnp.where(c == 1, ids[-16:], ids[:16])
    ids = cat(ids, round_ring(end, -1))
    far, other = send(ids, dz=4), send(ids, dc=1)

    widths = [share * len(g) for g in (FIRST, SECOND)]
    far, other, a1, a2, a3 = lax.optimization_barrier((far, other, a1, a2, a3))
    far_other = send(far, dc=1)
    xs = pl.pallas_call(
        stem_kernel,
        in_specs=[SMEM] + [VMEM] * 5,
        out_shape=[shape(4 * n_pos, n) for n in widths for _ in range(3)],
        scratch_shapes=[pltpu.VMEM((4 * n_pos + 16, patch), F32)],
        compiler_params=params(),
        cost_estimate=cost(4 * 10**9, 8 << 20),
    )(place, stem_weight, ids, far, other, far_other)

    r = send(pack(core, a1, a2, a3), dc=1)
    b1, b3 = cores(r, "x", "z", 1), cores(r, "x", "z", -1)
    last = cores(pick(core, [r], 3 * share, False), "x", "z", 2)
    cot = cotangent[0]
    cot_far = send(cot, dc=1)

    acc = conv1(core, xs[:3], [own, a1, a2, a3, r])
    b1, b3, last, acc = lax.optimization_barrier((b1, b3, last, acc))
    pieces = [b1, b3, send(pick(core, [b1, b3], 3 * share, True), dc=1), last]
    f_recv = send(conv2(core, acc, xs[3:], pieces, 0), dc=1)
    f_keep = conv2(core, acc, xs[3:], pieces, 1)
    q_mine, q_send, kv = project(core, f_keep, f_recv, query_weight, key_weight, value_weight.T)

    r1, r2 = round_ring(kv), round_ring(kv, -1)
    qs = [q_mine, send(q_send, dc=1)]
    state = attend(qs, [[kv], [send(kv, dc=1)]], (), False)
    r1, r2, *state = lax.optimization_barrier((r1, r2, *state))
    rr = round_ring(r1)
    r1_o, r2_o = send(r1, dc=1), send(r2, dc=1)
    state = attend(qs, [[r1], [r2]], state, False)
    state = attend(qs, [[r1_o], [r2_o]], state, False)
    rr, *state = lax.optimization_barrier((rr, *state))
    attn = attend(qs, [[rr], [send(rr, dc=1)]], state, True)

    own_part, *parts = gradient(at, cot, cot_far, attn)
    came = [cores(parts[k - 1], "x", "y", k) for k in (2, 1, 3)]
    attn, *_ = lax.optimization_barrier((attn, parts[0]))
    theirs = send(attn[n_pos:], dc=1)
    layer_out = finish(core, f_keep, f_recv, attn, theirs, out_weight)
    layer_out, *came = lax.optimization_barrier((layer_out, *came))
    chunks = chunks_of(at, own_part, came)
    groups = [[flat(i, j, k, 0) for j in range(NY) for k in range(NZ)] for i in range(NX)]
    groups += [[flat(i, j, k, 1) for i in range(NX) for k in range(NZ)] for j in range(NY)]
    came = lax.all_to_all(chunks, ("dp", "seq"), 0, 0, axis_index_groups=groups)
    keep, away = gathered(core, came)
    away = send(away, dc=1)
    out_grad = join(core, keep, away)
    return (layer_out[None], out_grad)


def solution(mesh):
    placed = (P("dp", "seq"), P(), P(None, "dp", None), P(), P(), P(), P(), P("dp", "seq", None))
    return jax.shard_map(
        local,
        mesh=mesh,
        in_specs=placed,
        out_specs=(P("dp", "seq", None), P(("dp", "seq"), None)),
        check_vma=False,
    )
```

```python
import functools
import math

import jax
import jax.numpy as jnp
from jax import lax
from jax.experimental import pallas as pl
from jax.experimental.pallas import tpu as pltpu
from jax.sharding import PartitionSpec as P

HEADS = 4
HQK = 128
HV = 192
STEP = 4
NX, NY, NZ = 4, 4, 8
BF = jnp.bfloat16
F32 = jnp.float32

FIRST = ((0, 0), (3, 0), (1, 0), (2, 0), (0, 3), (0, 1), (0, 2))
SECOND = ((3, 2), (3, 3), (3, 1), (1, 2), (1, 3), (1, 1), (2, 3), (2, 1), (2, 2))


def flat(x, y, z, c):
    return (x * 4 + z % 4) * 16 + y * 4 + (z // 4) * 2 + c


def route(value, target):
    places = [(x, y, z, c) for x in range(NX) for y in range(NY) for z in range(NZ) for c in range(2)]
    pairs = [(flat(*p), flat(*target(*p))) for p in places if target(*p)]
    return lax.ppermute(value, ("dp", "seq"), pairs)


def send(value, dx=0, dy=0, dz=0, dc=0):
    return route(
        value, lambda x, y, z, c: ((x + dx) % NX, (y + dy) % NY, (z + dz) % NZ, c ^ dc)
    )


def cores(value, first, second, by):
    def target(x, y, z, c):
        to = {"x": x, "y": y, "z": z}
        axis = (first, second)[c]
        step = -by if axis == "z" and by == 2 and z % 2 else by
        to[axis] = (to[axis] + step) % {"x": NX, "y": NY, "z": NZ}[axis]
        return to["x"], to["y"], to["z"], c

    return route(value, target)


def round_ring(value, up=1):
    return route(value, lambda x, y, z, c: (x, (y + up * (1 - 2 * c)) % NY, z, c))


def dot(a, b):
    return jnp.dot(a, b, preferred_element_type=F32)


def dot_t(a, b):
    return lax.dot_general(a, b, (((1,), (1,)), ((), ())), preferred_element_type=F32)


def params():
    return pltpu.CompilerParams(vmem_limit_bytes=20 << 20)


def cost(flops, moved=1 << 20, exps=0):
    return pl.CostEstimate(flops=flops, bytes_accessed=moved, transcendentals=exps)


SMEM = pl.BlockSpec(memory_space=pltpu.SMEM)
VMEM = pl.BlockSpec(memory_space=pltpu.VMEM)


def shape(*dims, dtype=BF):
    return jax.ShapeDtypeStruct(dims, dtype)


def stem_kernel(place, sw_ref, ids_ref, far_ref, other_ref, far_other_ref, *rest):
    outs, ext = rest[:-1], rest[-1]
    refs = (ids_ref, far_ref, other_ref, far_other_ref)
    x, z_lo, y, zh, c = [place[i] for i in range(5)]
    n_rows, d0 = sw_ref.shape
    share = d0 // (len(FIRST) + len(SECOND))
    to = lax.broadcasted_iota(jnp.int32, (n_rows, n_rows), 0)
    of = lax.broadcasted_iota(jnp.int32, (n_rows, n_rows), 1)
    patch = n_rows // 4
    rows = jnp.where(of == (to % patch) * 4 + to // patch, 1.0, 0.0).astype(BF)
    sw = dot(rows, sw_ref[...]).astype(BF)
    ordered = []
    for group in (FIRST, SECOND):
        n = share * len(group)
        lane = lax.broadcasted_iota(jnp.int32, (1, n), 1)
        wanted = jnp.zeros((1, n), jnp.int32)
        for i, (near, across) in enumerate(group):
            ox, oz = jnp.where(c == 0, near, across), jnp.where(c == 0, across, near)
            start = ((x + ox) % 4 * 4 + (z_lo + oz) % 4) * share
            here = (lane >= i * share) & (lane < (i + 1) * share)
            wanted = jnp.where(here, start + lane - i * share, wanted)
        chan = lax.broadcasted_iota(jnp.int32, (d0, n), 0)
        ordered.append(dot(sw, jnp.where(chan == wanted, 1.0, 0.0).astype(BF)).astype(BF))
    n_pos = refs[0].shape[0] - 16
    edge = jnp.full((STEP, ext.shape[1]), -1.0, F32)
    first = last = edge
    for i in range(4):
        came = refs[i][n_pos:, :].astype(F32)
        first = jnp.where((y > 0) & (2 * (1 - c) + 1 - zh == i), came[16 - STEP :], first)
        last = jnp.where((y < NY - 1) & (2 * c + zh == i), came[:STEP], last)
    ext[0:8, :] = jnp.concatenate([edge, first])
    ext[8 + 4 * n_pos :, :] = jnp.concatenate([last, edge])
    blocks = [zh * 2 + c, (1 - zh) * 2 + c, zh * 2 + 1 - c, (1 - zh) * 2 + 1 - c]
    for i, b in enumerate(blocks):
        block = refs[i][:n_pos, :]
        ext[pl.ds(pl.multiple_of(8 + b * n_pos, 8), n_pos), :] = block.astype(F32)
    n = n_pos + 16
    for i, b in enumerate(blocks[2:] + blocks[:2]):
        ids = ext[pl.ds(pl.multiple_of(b * n_pos, 8), n), :]
        onehot = jnp.concatenate(
            [jnp.where(ids == k, 1.0, 0.0).astype(BF) for k in range(4)], axis=1
        )
        for g, weight in enumerate(ordered):
            stem = jax.nn.gelu(dot(onehot, weight))
            for t in range(3):
                at = STEP * (t + 1)
                outs[g * 3 + t][i * n_pos : (i + 1) * n_pos, :] = stem[at : at + n_pos].astype(BF)


def tap_weights(pieces, t):
    share = pieces[0].shape[0] // 3
    return jnp.concatenate([p[t * share : (t + 1) * share] for p in pieces])


def pack_kernel(sel, a1, a2, a3, out):
    n, half = a1.shape[0], out.shape[1]
    other = pl.ds(pl.multiple_of((1 - sel[0]) * half, half), half)
    out[:n, :] = a2[:, :half]
    out[n : 2 * n, :] = a2[:, half:]
    out[2 * n : 3 * n, :] = a1[:, other]
    out[3 * n :, :] = a3[:, other]


def pack(c, a1, a2, a3):
    rows, width = a1.shape
    return pl.pallas_call(
        pack_kernel,
        in_specs=[SMEM] + [VMEM] * 3,
        out_shape=shape(4 * rows, width // 2),
        compiler_params=params(),
        cost_estimate=cost(0),
    )(c, a1, a2, a3)


def pick_kernel(flip, sel, *refs):
    ins, out = refs[:-1], refs[-1]
    n = out.shape[0] // len(ins)
    k = 1 - sel[0] if flip else sel[0]
    for i, ref in enumerate(ins):
        out[i * n : (i + 1) * n, :] = ref[pl.ds(pl.multiple_of(k * n, 16), n), :]


def pick(c, arrays, n, flip):
    return pl.pallas_call(
        functools.partial(pick_kernel, flip),
        in_specs=[SMEM] + [VMEM] * len(arrays),
        out_shape=shape(n * len(arrays), arrays[0].shape[1]),
        compiler_params=params(),
        cost_estimate=cost(0),
    )(c, *arrays)


def conv1_kernel(sel, x0, x1, x2, own, a1, a2, a3, r, out):
    n, half = own.shape[0], out.shape[1]
    mine = pl.ds(pl.multiple_of(sel[0] * half, half), half)
    pieces = [own[:, mine], a1[:, mine], a3[:, mine], a2[:, mine]]
    pieces += [r[2 * n : 3 * n, :], r[3 * n :, :], r[pl.ds(pl.multiple_of(sel[0] * n, 16), n), :]]
    step = x0.shape[0] // 4

    def body(i, _):
        here = pl.ds(pl.multiple_of(i * step, step), step)
        total = None
        for t, x in enumerate((x0, x1, x2)):
            part = dot(x[here, :], tap_weights(pieces, t))
            total = part if total is None else total + part
        out[here, :] = total
        return 0

    lax.fori_loop(0, 4, body, 0)


def conv2_kernel(part, sel, acc, x0, x1, x2, b1, b3, swapped, last, out):
    n = last.shape[0]
    mine = pl.ds(pl.multiple_of(sel[0] * n, 16), n)
    pieces = []
    for b in (b1, b3):
        pieces += [b[mine, :], b[2 * n : 3 * n, :], b[3 * n :, :]]
    pieces += [swapped[:n, :], swapped[n:, :], last[...]]
    rows = out.shape[0] // 2
    for i in range(2):
        here = pl.ds((2 * part + i) * rows, rows)
        total = acc[here, :]
        for t, x in enumerate((x0, x1, x2)):
            total = total + dot(x[here, :], tap_weights(pieces, t))
        out[i * rows : (i + 1) * rows, :] = jax.nn.gelu(total).astype(BF)


def conv1(c, xs, pieces):
    rows, cols = xs[0].shape[0], pieces[0].shape[1] // 2
    return pl.pallas_call(
        conv1_kernel,
        in_specs=[SMEM] + [VMEM] * 8,
        out_shape=shape(rows, cols, dtype=F32),
        compiler_params=params(),
        cost_estimate=cost(6 * rows * xs[0].shape[1] * cols, 7 << 20),
    )(c, *xs, *pieces)


def conv2(c, acc, xs, pieces, part):
    rows, cols = acc.shape
    return pl.pallas_call(
        functools.partial(conv2_kernel, part),
        in_specs=[SMEM] + [VMEM] * 8,
        out_shape=shape(rows // 2, cols),
        compiler_params=params(),
        cost_estimate=cost(3 * rows * xs[0].shape[1] * cols, 4 << 20),
    )(c, acc, *xs, *pieces)


def project_kernel(sel, fk, fr, wq, wk, wv, q_mine, message, kv_out):
    n_pos, half, qc = fk.shape[0] // 2, fk.shape[1], wq.shape[1] // 2
    c = sel[0]
    my, other = [pl.ds(pl.multiple_of(k * half, half), half) for k in (c, 1 - c)]
    mine, theirs = [pl.ds(pl.multiple_of(k * qc, qc), qc) for k in (c, 1 - c)]
    wide_k, wide_r = fk[...].astype(F32), fr[...].astype(F32)
    squares = jnp.sum(wide_k * wide_k, -1, keepdims=True)
    squares = squares + jnp.sum(wide_r * wide_r, -1, keepdims=True)
    scale = lax.rsqrt(squares / (2 * half) + 1e-06)
    nk, nr = (wide_k * scale).astype(BF), (wide_r * scale).astype(BF)
    factor = HQK ** (-0.5) * math.log2(math.e)
    hk, hr = nk[:n_pos], nr[:n_pos]
    q = ((dot(hk, wq[my, theirs]) + dot(hr, wq[other, theirs])) * factor).astype(BF)
    for h in range(qc // HQK):
        at = (5 + h) * n_pos
        message[at : at + n_pos, :] = q[:, h * HQK : (h + 1) * HQK]
    q_mine[...] = ((dot(hk, wq[my, mine]) + dot(hr, wq[other, mine])) * factor).astype(BF)
    n = 2 * n_pos
    kv_out[:n, :] = (dot(nk, wk[my, :]) + dot(nr, wk[other, :])).astype(BF)
    v = dot_t(nk, wv[:, my]) + dot_t(nr, wv[:, other])
    kv_out[n : 2 * n, :] = v[:, :128].astype(BF)
    tail = v[:, 128:]
    kv_out[2 * n :, :] = jnp.concatenate([tail[:n_pos], tail[n_pos:]], axis=1).astype(BF)
    message[: 5 * n_pos, :] = kv_out[...]


def project(c, f_keep, f_recv, query_weight, key_weight, value_weight):
    n, half = f_keep.shape
    n_pos = n // 2
    qc = query_weight.shape[1] // 2
    return pl.pallas_call(
        project_kernel,
        in_specs=[SMEM] + [VMEM] * 5,
        out_shape=[shape(n_pos, qc), shape(7 * n_pos, 128), shape(5 * n_pos, 128)],
        compiler_params=params(),
        cost_estimate=cost(4 * n * half * 640, 4 << 20),
    )(c, f_keep, f_recv, query_weight, key_weight, value_weight)


def unpack(packed):
    n = packed.shape[0] // 5
    k, va, tail = packed[: 2 * n], packed[2 * n : 4 * n], packed[4 * n :]
    tail = tail.astype(F32)
    tail = jnp.concatenate([tail, pltpu.roll(tail, 64, 1)])
    lane = lax.broadcasted_iota(jnp.int32, tail.shape, 1)
    tail = jnp.where(lane < HV - 128, tail, jnp.where(lane == HV - 128, 1.0, 0.0))
    return k, jnp.concatenate([va, tail.astype(BF)], axis=1)


def attend_kernel(groups, first, last, *refs):
    qs = refs[:2]
    at = 2
    kvs = []
    for n in groups:
        kvs.append(unpack(refs[at][: 5 * qs[0].shape[0], :]))
        at += n
    rest = refs[at:]
    if not first:
        m_in, acc_in = rest[:2]
        rest = rest[2:]
    rows = qs[0].shape[0]
    for w in range(2):
        for h in range(HEADS // 2):
            if w == 0:
                q = qs[0][:, h * HQK : (h + 1) * HQK]
            else:
                q = qs[1][(5 + h) * rows : (6 + h) * rows, :]
            scores = [dot_t(q, k) for k, _ in kvs]
            top = functools.reduce(
                jnp.maximum, [jnp.max(s, axis=1, keepdims=True) for s in scores]
            )
            here = pl.ds((w * 2 + h) * rows, rows)
            if not first:
                before = m_in[here, :1]
                top = jnp.maximum(top, before)
            total = None
            for s, (_, v) in zip(scores, kvs):
                part = dot(jnp.exp2(s - top).astype(BF), v)
                total = part if total is None else total + part
            if not first:
                total = total + acc_in[here, :] * jnp.exp2(before - top)
            if last:
                norm = total[:, :HV] / total[:, HV : HV + 1]
                rest[0][w * rows : (w + 1) * rows, h * HV : (h + 1) * HV] = norm.astype(BF)
            else:
                rest[0][here, :] = jnp.broadcast_to(top, (rows, 128))
                rest[1][here, :] = total


def attend(qs, kvs, state, last):
    rows = qs[0].shape[0]
    if last:
        out = shape(2 * rows, HEADS // 2 * HV)
    else:
        out = (shape(4 * rows, 128, dtype=F32), shape(4 * rows, 256, dtype=F32))
    n = sum(kv.shape[0] for group in kvs for kv in group) * 2 // 5
    return pl.pallas_call(
        functools.partial(attend_kernel, tuple(len(g) for g in kvs), not state, last),
        out_shape=out,
        compiler_params=params(),
        cost_estimate=cost(0),
    )(*qs, *[kv for group in kvs for kv in group], *state)


def finish_kernel(sel, fk, fr, attn, theirs, w, out):
    n_pos, cols = theirs.shape
    half = fk.shape[1]
    c = sel[0]
    mine, other = [pl.ds(pl.multiple_of(k * cols, cols), cols) for k in (c, 1 - c)]
    a, b = attn[:n_pos, :], theirs[...]
    ours, far = fk[:n_pos, :].astype(F32), fr[:n_pos, :].astype(F32)
    for k in range(2):
        rows = slice(k * half, (k + 1) * half)
        total = jnp.where(c == k, ours, far) + dot_t(a, w[rows, mine]) + dot_t(b, w[rows, other])
        out[:, rows] = total.astype(BF)


def finish(c, f_keep, f_recv, attn, theirs, out_weight):
    n_pos, cols = theirs.shape
    width = out_weight.shape[0]
    return pl.pallas_call(
        finish_kernel,
        in_specs=[SMEM] + [VMEM] * 5,
        out_shape=shape(n_pos, width),
        compiler_params=params(),
        cost_estimate=cost(4 * n_pos * width * cols, 4 << 20),
    )(c, f_keep, f_recv, attn, theirs, out_weight)


def grad_kernel(at, cot, cot_far, attn, own, one, two, three, total):
    n_pos, block = cot.shape[0], cot.shape[1] // 4
    a, b = attn[:n_pos, :], attn[n_pos:, :]
    down = lambda u, v: lax.dot_general(u, v, (((0,), (0,)), ((), ())), preferred_element_type=F32)
    for k in range(4):
        here = slice(k * block, (k + 1) * block)
        total[here, :] = down(cot[:, here], a) + down(cot_far[:, here], b)
    n = block // 16
    for k, out in enumerate((own, one, two, three)):
        x, y = (at[0] + k) % 4, (at[1] + k) % 4
        for i in range(16):
            start = jnp.where(at[2] == 0, x * block + i * n, i * 4 * n + y * n)
            rows = pl.ds(pl.multiple_of(start, 8), n)
            out[i * n : (i + 1) * n, :] = total[rows, :].astype(out.dtype)


def quarters(rows, cols):
    return [shape(rows, cols, dtype=F32)] + [shape(rows, cols)] * 3


def gradient(at, cot, cot_far, attn):
    block, cols = cot.shape[1] // 4, attn.shape[1]
    return pl.pallas_call(
        grad_kernel,
        in_specs=[SMEM] + [VMEM] * 3,
        out_shape=quarters(block, cols),
        scratch_shapes=[pltpu.VMEM((cot.shape[1], cols), F32)],
        compiler_params=params(),
        cost_estimate=cost(16 * cot.shape[0] * block * cols, 3 << 20),
    )(at, cot, cot_far, attn)


def chunks_kernel(at, own, a, b, d, out, total):
    total[...] = own[...] + a[...].astype(F32) + b[...].astype(F32) + d[...].astype(F32)
    n = out.shape[1]
    for j in range(4):
        for zl in range(4):
            start = jnp.where(at[2] == 0, zl * 4 + j, j * 4 + zl) * 2 * n
            rows = total[pl.ds(pl.multiple_of(start, 8), 2 * n), :].astype(BF)
            out[j * 8 + zl] = rows[:n]
            out[j * 8 + 4 + zl] = rows[n:]


def chunks_of(at, own, came):
    rows, cols = own.shape
    return pl.pallas_call(
        chunks_kernel,
        in_specs=[SMEM] + [VMEM] * 4,
        out_shape=shape(32, rows // 32, cols),
        scratch_shapes=[pltpu.VMEM((rows, cols), F32)],
        compiler_params=params(),
        cost_estimate=cost(rows * cols * 4),
    )(at, own, *came)


def gather_kernel(sel, came, keep, away):
    total = jnp.sum(came[...].astype(F32), axis=0)
    n = total.shape[0] // 2
    keep[...] = jnp.where(sel[0] == 0, total[:n], total[n:])
    away[...] = jnp.where(sel[0] == 0, total[n:], total[:n])


def gathered(c, came):
    _, rows, cols = came.shape
    return pl.pallas_call(
        gather_kernel,
        in_specs=[SMEM, VMEM],
        out_shape=[shape(rows // 2, cols, dtype=F32)] * 2,
        compiler_params=params(),
        cost_estimate=cost(rows * cols * 32),
    )(c, came)


def join_kernel(sel, keep, away, out):
    cols = keep.shape[1]
    out[:, :cols] = jnp.where(sel[0] == 0, keep[...], away[...])
    out[:, cols:] = jnp.where(sel[0] == 0, away[...], keep[...])


def join(c, keep, away):
    rows, cols = keep.shape
    return pl.pallas_call(
        join_kernel,
        in_specs=[SMEM] + [VMEM] * 2,
        out_shape=shape(rows, 2 * cols, dtype=F32),
        compiler_params=params(),
        cost_estimate=cost(0),
    )(c, keep, away)


def local(
    dna_ids,
    stem_weight,
    kernel_taps_weight,
    query_weight,
    key_weight,
    value_weight,
    out_weight,
    cotangent,
):
    patch = stem_weight.shape[0] // 4
    n_pos = dna_ids.shape[1] // patch
    share, width = kernel_taps_weight.shape[1:]
    dp, seq = lax.axis_index("dp"), lax.axis_index("seq")
    x, zl = dp // 4, dp % 4
    y, zh, c = seq // 4, (seq // 2) % 2, seq % 2
    core = c.astype(jnp.int32).reshape(1)
    place = jnp.stack([x, zl, y, zh, c]).astype(jnp.int32)
    at = jnp.stack([x, y, c]).astype(jnp.int32)
    core, place, at, dna_ids = lax.optimization_barrier((core, place, at, dna_ids))
    cat = lambda *a: jnp.concatenate(a)

    own = kernel_taps_weight.reshape(3 * share, width)
    a1, a3, a2 = [cores(own, "x", "z", k) for k in (1, -1, 2)]

    ids = lax.optimization_barrier(dna_ids.reshape(n_pos, patch).astype(BF))
    end = jnp.where(c == 1, ids[-16:], ids[:16])
    ids = cat(ids, round_ring(end, -1))
    far, other = send(ids, dz=4), send(ids, dc=1)

    widths = [share * len(g) for g in (FIRST, SECOND)]
    far, other, a1, a2, a3 = lax.optimization_barrier((far, other, a1, a2, a3))
    far_other = send(far, dc=1)
    xs = pl.pallas_call(
        stem_kernel,
        in_specs=[SMEM] + [VMEM] * 5,
        out_shape=[shape(4 * n_pos, n) for n in widths for _ in range(3)],
        scratch_shapes=[pltpu.VMEM((4 * n_pos + 16, patch), F32)],
        compiler_params=params(),
        cost_estimate=cost(4 * 10**9, 8 << 20),
    )(place, stem_weight, ids, far, other, far_other)

    r = send(pack(core, a1, a2, a3), dc=1)
    b1, b3 = cores(r, "x", "z", 1), cores(r, "x", "z", -1)
    last = cores(pick(core, [r], 3 * share, False), "x", "z", 2)
    cot = cotangent[0]
    cot_far = send(cot, dc=1)

    acc = conv1(core, xs[:3], [own, a1, a2, a3, r])
    b1, b3, last, acc = lax.optimization_barrier((b1, b3, last, acc))
    pieces = [b1, b3, send(pick(core, [b1, b3], 3 * share, True), dc=1), last]
    f_recv = send(conv2(core, acc, xs[3:], pieces, 0), dc=1)
    f_keep = conv2(core, acc, xs[3:], pieces, 1)
    q_mine, message, kv = project(core, f_keep, f_recv, query_weight, key_weight, value_weight.T)

    r1, r2 = round_ring(kv), round_ring(kv, -1)
    qs = [q_mine, send(message, dc=1)]
    state = attend(qs, [[kv], [qs[1]]], (), False)
    r1, r2, *state = lax.optimization_barrier((r1, r2, *state))
    rr = round_ring(r1)
    r1_o, r2_o = send(r1, dc=1), send(r2, dc=1)
    state = attend(qs, [[r1], [r2]], state, False)
    state = attend(qs, [[r1_o], [r2_o]], state, False)
    rr, *state = lax.optimization_barrier((rr, *state))
    attn = attend(qs, [[rr], [send(rr, dc=1)]], state, True)

    own_part, *parts = gradient(at, cot, cot_far, attn)
    came = [cores(parts[k - 1], "x", "y", k) for k in (2, 1, 3)]
    attn, *_ = lax.optimization_barrier((attn, parts[0]))
    theirs = send(attn[n_pos:], dc=1)
    layer_out = finish(core, f_keep, f_recv, attn, theirs, out_weight)
    layer_out, *came = lax.optimization_barrier((layer_out, *came))
    chunks = chunks_of(at, own_part, came)
    groups = [[flat(i, j, k, 0) for j in range(NY) for k in range(NZ)] for i in range(NX)]
    groups += [[flat(i, j, k, 1) for i in range(NX) for k in range(NZ)] for j in range(NY)]
    came = lax.all_to_all(chunks, ("dp", "seq"), 0, 0, axis_index_groups=groups)
    keep, away = gathered(core, came)
    away = send(away, dc=1)
    out_grad = join(core, keep, away)
    return (layer_out[None], out_grad)


def solution(mesh):
    placed = (P("dp", "seq"), P(), P(None, "dp", None), P(), P(), P(), P(), P("dp", "seq", None))
    return jax.shard_map(
        local,
        mesh=mesh,
        in_specs=placed,
        out_specs=(P("dp", "seq", None), P(("dp", "seq"), None)),
        check_vma=False,
    )
```
